128 devices in a mesh: ctx: 32 (over y, z_lo, x), dp: 4 (over z_hi, core).
Axes of the slice: x: 4, y: 4, z: 4 (z_hi: 2, z_lo: 2; z = z_hi * 2 + z_lo), core: 2. Of those that a mesh axis runs over, the one named last changes fastest.
Arguments:
- q_proj: bfloat16 [4, 2, 2048, 1792], P('dp', None, 'ctx'), may hold values from -240 to 240
- k_proj: bfloat16 [4, 2, 2048, 256], P('dp', None, 'ctx'), may hold values from -12 to 12
- v_proj: bfloat16 [4, 2, 2048, 256], P('dp', None, 'ctx'), may hold values from -6 to 6
- q_bias: float32 [1792], replicated, may hold values from -4 to 4
- v_bias: float32 [256], replicated, may hold values from -2.5 to 2.5
- cotangent: bfloat16 [4, 2, 2048, 1792], P('dp', None, 'ctx'), may hold values from -6 to 6
- lengths: int32 [4, 16], P('dp'), may hold values from 1 to 1024, 4096 in all within a row
Outputs:
- attended: bfloat16 [4, 2, 2048, 1792], P('dp', None, 'ctx')
- q_grad: bfloat16 [4, 2, 2048, 1792], P('dp', None, 'ctx')
- k_grad: bfloat16 [4, 2, 2048, 256], P('dp', None, 'ctx')
- v_grad: bfloat16 [4, 2, 2048, 256], P('dp', None, 'ctx')
- q_bias_grad: float32 [1792], replicated
- v_bias_grad: float32 [256], replicated
The draws below stay inside these ranges and needn't reach their ends.
Inputs may be any that keep to these rules, and one draw needn't show every extreme that they name: `lengths`: each row sums to 4096; the longest document of each row has exactly 1024 tokens.
All inputs are finite; a program needn't handle non-finite values.
Results may differ from the reference program's by a relative error of at most 0.012.
Values may be sent and summed in bfloat16 or wider, within the bound.
No kernel may reach another device: no remote copies, remote signals or barrier semaphores. Data moves between devices by JAX's collectives and lax.ppermute only.
A program may use at most 192 MiB of HBM per device.

```python
import math
import jax
import jax.numpy as jnp
import numpy as np
from jax import lax

HD = 128
KVH = 2
GROUP = 7
HQ = 1792
KW = 256
BLOCK_TOK = 64
SEQ = 4096
HALF = 2048
SEQS = 4
NDOC = 16
MOST = 1024
TILE = 512
N_CTX = 32


def shared_keys(key):
    normal_rows = jnp.clip(jax.random.normal(jax.random.fold_in(key, 11), (SEQS, 2, HALF, KW), jnp.float32), -6.0, 6.0)
    return normal_rows


def draw_k_proj(key, part):
    normal_rows = shared_keys(key)
    return normal_rows.astype(jnp.bfloat16)


def draw_q_proj(key, part):
    normal_rows = 2.0 * jnp.clip(jax.random.normal(jax.random.fold_in(key, 21), (SEQS, 2, HALF, HQ), jnp.float32), -6.0, 6.0)
    return normal_rows.astype(jnp.bfloat16)


def block_scale(rng, extent, cuts, low, largest):
    gain, own = 1.0, jax.random.fold_in(rng, 6)
    for axis_at, parts in cuts:
        steps = jnp.exp(jax.random.uniform(jax.random.fold_in(own, axis_at), (parts,), jnp.float32, low / len(cuts), largest / len(cuts)))
        gain = gain * jnp.repeat(steps, extent[axis_at] // parts).reshape([-1 if axis == axis_at else 1 for axis in range(len(extent))])
    return gain


def split_up(count, total, bound, lean):
    portions = [(1 << 20) // math.isqrt(standing ** lean) + 1 for standing in range(2, count + 1)]
    spare, counts = total - bound - (count - 1), [1] * (count - 1)
    while spare > 0:
        free = [i for i in range(count - 1) if counts[i] < bound]
        mass, remaining = sum([portions[i] for i in free]), spare
        for i in free:
            more = min(bound - counts[i], max(1, remaining * portions[i] // mass), spare)
            counts[i] = counts[i] + more
            spare = spare - more
    return np.array([bound] + counts)


def ragged_sizes(stream_key, count, total, reach, skew):
    if count == 2:
        one = jax.random.randint(stream_key, (), max(1, total - reach), min(reach, total - 1) + 1)
        return jnp.stack([one, total - one])
    sizes = jnp.asarray(split_up(count, total, reach, skew), jnp.int32)
    twos = (count - 1) // 2
    source_of, sink = sizes[1:1 + 2 * twos:2], sizes[2:2 + 2 * twos:2]
    room = jnp.minimum(source_of - 1, reach - sink)
    moved = jax.random.randint(jax.random.fold_in(stream_key, 1), (twos,), 0, 1 << 20) % (room + 1)
    sizes = sizes.at[1:1 + 2 * twos:2].set(source_of - moved).at[2:2 + 2 * twos:2].set(sink + moved)
    return sizes[jax.random.permutation(jax.random.fold_in(stream_key, 2), count)]


def normal_values(rng, extent, deviation, most, cuts=(), held_as=jnp.bfloat16):
    level = block_scale(rng, extent, cuts, -0.22, 0.18) if cuts else 1.0
    entries = jax.random.normal(rng, extent, jnp.float32) * deviation * level
    return jnp.minimum(jnp.maximum(entries, -most), most).astype(held_as)


def setup_inputs(seed: int = 0) -> dict:
    keys = jax.random.split(jax.random.key(seed), 8)
    return {
        "q_proj": draw_q_proj(jax.random.fold_in(keys[7], 71), 0),
        "k_proj": draw_k_proj(jax.random.fold_in(keys[7], 71), 0),
        "v_proj": normal_values(keys[2], (SEQS, 2, HALF, KW), 1.0, 6.0, ((0, 4), (2, 32))),
        "q_bias": normal_values(keys[3], (HQ,), 1.0, 4.0, (), jnp.float32),
        "v_bias": normal_values(keys[4], (KW,), 0.5, 2.5, (), jnp.float32),
        "cotangent": normal_values(keys[5], (SEQS, 2, HALF, HQ), 1.0, 6.0, ((0, 4), (2, 32))),
        "lengths": jax.vmap(lambda own: ragged_sizes(own, NDOC, SEQ, MOST, 2))(jax.random.split(keys[6], SEQS)).reshape((SEQS, NDOC)).astype(jnp.int32),
    }


MASKED = -1e+30

def unfold(folded):
    front = folded[0]
    later = folded[1].reshape(N_CTX, BLOCK_TOK, -1)[::-1].reshape(HALF, -1)
    return jnp.concatenate([front, later], axis=0)

def refold(natural):
    front = natural[:HALF]
    later = natural[HALF:].reshape(N_CTX, BLOCK_TOK, -1)[::-1].reshape(HALF, -1)
    return jnp.stack([front, later])

def barrier_round(values):
    return lax.optimization_barrier(values.astype(jnp.bfloat16)).astype(jnp.float32)

def one_sequence(q_proj, k_proj, v_proj, q_bias, v_bias, cotangent, lengths):
    score_scale = 1.0 / math.sqrt(HD)
    query_rows = unfold(barrier_round(q_proj.astype(jnp.float32) + q_bias))
    key_rows = unfold(k_proj).astype(jnp.float32).reshape(SEQ, KVH, HD)
    value_rows = unfold(barrier_round(v_proj.astype(jnp.float32) + v_bias)).reshape(SEQ, KVH, HD)
    cot_rows = unfold(cotangent).astype(jnp.float32)
    places = jnp.arange(SEQ, dtype=jnp.int32)
    doc_ends = jnp.cumsum(lengths).astype(jnp.int32)
    doc_ids = lax.optimization_barrier(jnp.sum((places[:, None] >= doc_ends[None, :]).astype(jnp.int32), axis=1))
    tile_count = SEQ // TILE
    query_tiles = query_rows.reshape(tile_count, TILE, KVH, GROUP, HD)
    cot_tiles = cot_rows.reshape(tile_count, TILE, KVH, GROUP, HD)
    pos_tiles = places.reshape(tile_count, TILE)
    doc_tiles = doc_ids.reshape(tile_count, TILE)

    def tile_step(carry, tile):
        key_grad, value_grad = carry
        query_tile, cot_tile, tile_pos, tile_doc = tile
        visible = (tile_doc[:, None] == doc_ids[None, :]) & (places[None, :] <= tile_pos[:, None])
        scores = jnp.einsum('tged,jgd->getj', query_tile, key_rows) * score_scale
        masked_scores = jnp.where(visible, scores, MASKED)
        row_top = lax.optimization_barrier(jnp.max(masked_scores, axis=-1))
        totals = lax.optimization_barrier(jnp.sum(jnp.where(visible, jnp.exp(masked_scores - row_top[..., None]), 0.0), axis=-1))
        log_total = row_top + jnp.log(totals)
        weights = jnp.exp(jnp.where(visible, scores - log_total[..., None], MASKED))
        weights_low = barrier_round(weights)
        summed = jnp.einsum('getj,jgd->tged', weights_low, value_rows)
        row_delta = jnp.einsum('tged,tged->get', cot_tile, summed)
        grad_weights = jnp.einsum('tged,jgd->getj', cot_tile, value_rows)
        grad_scores = barrier_round(weights * (grad_weights - row_delta[..., None]))
        query_grad = jnp.einsum('getj,jgd->tged', grad_scores, key_rows) * score_scale
        key_grad = key_grad + jnp.einsum('getj,tged->jgd', grad_scores, query_tile)
        value_grad = value_grad + jnp.einsum('getj,tged->jgd', weights_low, cot_tile)
        return ((key_grad, value_grad), (summed.astype(jnp.bfloat16).reshape(TILE, HQ), query_grad.reshape(TILE, HQ)))
    zero_keys = jnp.zeros((SEQ, KVH, HD), jnp.float32)
    (key_grad, value_grad), (attended, query_grad) = lax.scan(tile_step, (zero_keys, zero_keys), (query_tiles, cot_tiles, pos_tiles, doc_tiles))
    attended = attended.reshape(SEQ, HQ)
    query_grad = query_grad.reshape(SEQ, HQ)
    key_grad = key_grad.reshape(SEQ, KW) * score_scale
    value_grad = value_grad.reshape(SEQ, KW)
    return (refold(attended), refold(query_grad.astype(jnp.bfloat16)), refold(key_grad.astype(jnp.bfloat16)), refold(value_grad.astype(jnp.bfloat16)), lax.optimization_barrier(jnp.sum(query_grad, axis=0)), lax.optimization_barrier(jnp.sum(value_grad, axis=0)))

def reference(q_proj, k_proj, v_proj, q_bias, v_bias, cotangent, lengths):
    results = [one_sequence(q_proj[sequence], k_proj[sequence], v_proj[sequence], q_bias, v_bias, cotangent[sequence], lengths[sequence]) for sequence in range(SEQS)]
    attended = jnp.stack([entry[0] for entry in results])
    q_grad = jnp.stack([entry[1] for entry in results])
    k_grad = jnp.stack([entry[2] for entry in results])
    v_grad = jnp.stack([entry[3] for entry in results])
    q_bias_grad = results[0][4]
    v_bias_grad = results[0][5]
    for entry in results[1:]:
        q_bias_grad = q_bias_grad + entry[4]
        v_bias_grad = v_bias_grad + entry[5]
    return (attended, q_grad, k_grad, v_grad, q_bias_grad, v_bias_grad)
```

```python
import functools
import math

import jax
import jax.numpy as jnp
from jax import lax
from jax.experimental import pallas as pl
from jax.experimental.pallas import tpu as pltpu
from jax.sharding import PartitionSpec as P

HD = 128
KVH = 2
GROUP = 7
HQ = 1792
KW = 256
MOST = 1024

MASKED = -1e30
BLOCKS_PER_CHUNK = 4

NT = (((1,), (1,)), ((), ()))
NN = (((1,), (0,)), ((), ()))
TN = (((0,), (0,)), ((), ()))


def dot(a, b, dims):
    return lax.dot_general(a, b, dims, preferred_element_type=jnp.float32)


def attention_kernel(
    group_size,
    where_ref,
    len_ref,
    q_ref,
    ct_ref,
    qb_ref,
    kv_ref,
    att_ref,
    qg_ref,
    gr_ref,
    sum_ref,
    win_ref,
    q_rows,
    d_rows,
    p_ref,
    pb_ref,
    grad_ref,
    acc_ref,
):
    block_len = q_ref.shape[1]
    rows = GROUP * block_len
    chunk = BLOCKS_PER_CHUNK * block_len
    scale = 1.0 / math.sqrt(HD)
    log2e = 1.0 / math.log(2.0)
    last_block = 2 * group_size - 1
    me = where_ref[0]
    n_docs = len_ref.shape[1]

    gr_ref[...] = jnp.zeros_like(gr_ref)
    sum_ref[...] = jnp.zeros_like(sum_ref)

    def place(block):
        early = block < group_size
        return jnp.where(early, block, last_block - block), jnp.where(early, 0, 1)

    def query_block(h, carry):
        own = jnp.where(h == 0, me, last_block - me)
        first_pos = own * block_len
        token = lax.broadcasted_iota(jnp.int32, (1, rows), 1) % block_len
        query_pos = first_pos + token
        query_start = jnp.zeros_like(query_pos)
        end = jnp.int32(0)
        first_start = jnp.int32(0)
        for k in range(n_docs):
            end = end + len_ref[0, k]
            query_start = jnp.where(query_pos >= end, end, query_start)
            first_start = jnp.where(first_pos >= end, end, first_start)
        low = first_start // block_len
        n_blocks = own - low + 1
        n_chunks = (n_blocks + BLOCKS_PER_CHUNK - 1) // BLOCKS_PER_CHUNK

        def load(i, carry):
            c, half = place(jnp.minimum(low + i, own))
            win_ref[pl.ds(i * block_len, block_len), :] = kv_ref[c, half]
            return carry

        lax.fori_loop(0, n_chunks * BLOCKS_PER_CHUNK, load, 0)

        for g in range(KVH):
            for t in range(GROUP):
                f = (g * GROUP + t) * HD
                here = slice(t * block_len, (t + 1) * block_len)
                q_rows[here, :] = (
                    q_ref[h, :, f : f + HD].astype(jnp.float32) + qb_ref[:, f : f + HD]
                ).astype(jnp.bfloat16)
                d_rows[here, :] = ct_ref[h, :, f : f + HD]
            key_cols = slice(g * HD, (g + 1) * HD)
            value_cols = slice(KW + g * HD, KW + (g + 1) * HD)

            def score_step(i, top):
                at = pl.ds(pl.multiple_of(i * chunk, chunk), chunk)
                s = dot(win_ref[at, key_cols], q_rows[...], NT) * (scale * log2e)
                key_pos = (low * block_len + i * chunk) + lax.broadcasted_iota(
                    jnp.int32, (chunk, 1), 0
                )
                visible = (key_pos >= query_start) & (key_pos <= query_pos)
                s = jnp.where(visible, s, MASKED)
                p_ref[at, :] = s
                return jnp.maximum(top, jnp.max(s, axis=0, keepdims=True))

            top = lax.fori_loop(
                0, n_chunks, score_step, jnp.full((1, rows), MASKED, jnp.float32)
            )

            def exp_step(i, total):
                at = pl.ds(pl.multiple_of(i * chunk, chunk), chunk)
                e = jnp.exp2(p_ref[at, :] - top)
                p_ref[at, :] = e
                return total + jnp.sum(e, axis=0, keepdims=True)

            total = lax.fori_loop(0, n_chunks, exp_step, jnp.zeros((1, rows), jnp.float32))
            inverse = 1.0 / total

            acc_ref[...] = jnp.zeros_like(acc_ref)

            def out_step(i, carry):
                at = pl.ds(pl.multiple_of(i * chunk, chunk), chunk)
                p = p_ref[at, :] * inverse
                p_ref[at, :] = p
                low_p = p.astype(jnp.bfloat16)
                pb_ref[at, :] = low_p
                acc_ref[...] += dot(win_ref[at, value_cols], low_p, TN)
                return carry

            lax.fori_loop(0, n_chunks, out_step, 0)
            summed = acc_ref[...]
            delta = jnp.sum(
                summed * jnp.transpose(d_rows[...].astype(jnp.float32)), axis=0, keepdims=True
            )
            out_rows = jnp.transpose(summed).astype(jnp.bfloat16)
            for t in range(GROUP):
                f = (g * GROUP + t) * HD
                att_ref[h, :, f : f + HD] = out_rows[t * block_len : (t + 1) * block_len]

            acc_ref[...] = jnp.zeros_like(acc_ref)

            def grad_step(i, value_total):
                at = pl.ds(pl.multiple_of(i * chunk, chunk), chunk)
                dp = dot(win_ref[at, value_cols], d_rows[...], NT)
                ds = (p_ref[at, :] * (dp - delta)).astype(jnp.bfloat16)
                value_part = dot(pb_ref[at, :], d_rows[...], NN)
                grad_ref[at, value_cols] = value_part
                grad_ref[at, key_cols] = dot(ds, q_rows[...], NN) * scale
                acc_ref[...] += dot(win_ref[at, key_cols], ds, TN)
                return value_total + jnp.sum(value_part, axis=0, keepdims=True)

            value_total = lax.fori_loop(
                0, n_chunks, grad_step, jnp.zeros((1, HD), jnp.float32)
            )
            v_row = KVH * GROUP + g
            sum_ref[v_row : v_row + 1, :] += value_total
            query_grad = jnp.transpose(acc_ref[...] * scale)
            for t in range(GROUP):
                f = (g * GROUP + t) * HD
                part = query_grad[t * block_len : (t + 1) * block_len]
                qg_ref[h, :, f : f + HD] = part.astype(jnp.bfloat16)
                row = g * GROUP + t
                sum_ref[row : row + 1, :] += jnp.sum(part, axis=0, keepdims=True)

        def store(i, carry):
            c, half = place(low + i)
            part = grad_ref[pl.ds(i * block_len, block_len), :]
            gr_ref[c, half] = (gr_ref[c, half].astype(jnp.float32) + part).astype(jnp.bfloat16)
            return carry

        lax.fori_loop(0, n_blocks, store, 0)
        return carry

    lax.fori_loop(0, 2, query_block, 0)


def attention(group_size, me, lengths, q, ct, q_bias, kv):
    block_len = q.shape[1]
    rows = GROUP * block_len
    window = -(-(MOST // block_len + 1) // BLOCKS_PER_CHUNK) * BLOCKS_PER_CHUNK * block_len
    smem = pl.BlockSpec(memory_space=pltpu.SMEM)
    vmem = pl.BlockSpec(memory_space=pltpu.VMEM)
    return pl.pallas_call(
        functools.partial(attention_kernel, group_size),
        out_shape=(
            jax.ShapeDtypeStruct(q.shape, jnp.bfloat16),
            jax.ShapeDtypeStruct(q.shape, jnp.bfloat16),
            jax.ShapeDtypeStruct(kv.shape, jnp.bfloat16),
            jax.ShapeDtypeStruct((KVH * GROUP + KVH, HD), jnp.float32),
        ),
        in_specs=[smem, smem, vmem, vmem, vmem, vmem],
        out_specs=(vmem, vmem, vmem, vmem),
        scratch_shapes=[
            pltpu.VMEM((window, 2 * KW), jnp.bfloat16),
            pltpu.VMEM((rows, HD), jnp.bfloat16),
            pltpu.VMEM((rows, HD), jnp.bfloat16),
            pltpu.VMEM((window, rows), jnp.float32),
            pltpu.VMEM((window, rows), jnp.bfloat16),
            pltpu.VMEM((window, 2 * KW), jnp.float32),
            pltpu.VMEM((HD, rows), jnp.float32),
        ],
        compiler_params=pltpu.CompilerParams(vmem_limit_bytes=48 * 1024 * 1024),
        cost_estimate=pl.CostEstimate(
            flops=3_000_000_000, bytes_accessed=10_000_000, transcendentals=2_000_000
        ),
        name="attention",
    )(me, lengths, q, ct, q_bias, kv)


def all_sum(x, axes):
    for axis in axes:
        size = lax.axis_size(axis)
        step = 1
        while step < size:
            x = x + lax.ppermute(x, axis, [(i, i ^ step) for i in range(size)])
            step *= 2
    return x


def on_device(q_proj, k_proj, v_proj, q_bias, v_bias, cotangent, lengths):
    group_size = lax.axis_size("ctx")
    me = lax.axis_index("ctx").astype(jnp.int32)
    value_rows = (v_proj[0].astype(jnp.float32) + v_bias).astype(jnp.bfloat16)
    key_value = jnp.concatenate([k_proj[0], value_rows], axis=-1)
    sent = jnp.broadcast_to(key_value[None], (group_size, *key_value.shape))
    gathered = lax.all_to_all(sent, "ctx", 0, 0)
    attended, q_grad, parts, sums = attention(
        group_size, me[None], lengths, q_proj[0], cotangent[0], q_bias[None], gathered
    )
    returned = lax.all_to_all(parts, "ctx", 0, 0)
    totals = jnp.sum(returned.astype(jnp.float32), axis=0)
    k_grad = totals[..., :KW].astype(jnp.bfloat16)
    v_grad = totals[..., KW:].astype(jnp.bfloat16)
    sums = all_sum(sums, ("ctx", "dp"))
    return (
        attended[None],
        q_grad[None],
        k_grad[None],
        v_grad[None],
        sums[: KVH * GROUP].reshape(HQ),
        sums[KVH * GROUP :].reshape(KW),
    )


def solution(mesh):
    placed = (
        P("dp", None, "ctx", None),
        P("dp", None, "ctx", None),
        P("dp", None, "ctx", None),
        P(),
        P(),
        P("dp", None, "ctx", None),
        P("dp", None),
    )
    return jax.shard_map(
        on_device,
        mesh=mesh,
        in_specs=placed,
        out_specs=(
            P("dp", None, "ctx", None),
            P("dp", None, "ctx", None),
            P("dp", None, "ctx", None),
            P("dp", None, "ctx", None),
            P(),
            P(),
        ),
        check_vma=False,
    )
```

```python
import functools
import math

import jax
import jax.numpy as jnp
from jax import lax
from jax.experimental import pallas as pl
from jax.experimental.pallas import tpu as pltpu
from jax.sharding import PartitionSpec as P

HD = 128
KVH = 2
GROUP = 7
HQ = 1792
KW = 256
MOST = 1024

HALF_Q = GROUP * HD
SLOT_W = 2 * HD
SUM_ROWS = 16
MASKED = -1e30
VMEM_BYTES = 60 * 1024 * 1024
GOT_PARTS = 4
BLOCKS_PER_CHUNK = 4

NT = (((1,), (1,)), ((), ()))
NN = (((1,), (0,)), ((), ()))
TN = (((0,), (0,)), ((), ()))

SMEM = pl.BlockSpec(memory_space=pltpu.SMEM)
VMEM = pl.BlockSpec(memory_space=pltpu.VMEM)
HBM = pl.BlockSpec(memory_space=pltpu.HBM)


def dot(a, b, dims):
    return lax.dot_general(a, b, dims, preferred_element_type=jnp.float32)


def lanes(start, size):
    return pl.ds(pl.multiple_of(start, HD), size)


def send_kernel(group_size, me_ref, k_ref, v_ref, vb_ref, q_ref, ct_ref, send_ref, swap_ref, kv_ref, sem, swap_sem):
    block_len = k_ref.shape[1]
    other = 1 - me_ref[0] % 2
    copies = []
    for i, ref in enumerate((q_ref, ct_ref)):
        copies.append(
            pltpu.make_async_copy(
                ref.at[:, :, lanes(other * HALF_Q, HALF_Q)], swap_ref.at[i], swap_sem.at[i]
            )
        )
    for copy in copies:
        copy.start()
    for g in range(KVH):
        cols = slice(g * HD, (g + 1) * HD)
        for h in range(2):
            here = slice(h * block_len, (h + 1) * block_len)
            kv_ref[g, here, :HD] = k_ref[h, :, cols]
            kv_ref[g, here, HD:] = (
                v_ref[h, :, cols].astype(jnp.float32) + vb_ref[:, cols]
            ).astype(jnp.bfloat16)
    for d in range(group_size):
        copy = pltpu.make_async_copy(kv_ref.at[d % 2], send_ref.at[d], sem.at[d])
        copy.start()
        copies.append(copy)
    for copy in copies:
        copy.wait()


def attention_kernel(
    group_size,
    me_ref,
    len_ref,
    q_ref,
    ct_ref,
    other_hbm,
    qb_ref,
    kv_ref,
    mine_hbm,
    back_hbm,
    gr_ref,
    other_ref,
    mine_ref,
    back_ref,
    stage_ref,
    windows_ref,
    q_rows,
    d_rows,
    p_ref,
    grad_ref,
    acc_ref,
    row_ref,
    sum_ref,
    sems,
    load_sems,
):
    block_len = q_ref.shape[1]
    pair_len = 2 * block_len
    rows = GROUP * pair_len
    chunk = BLOCKS_PER_CHUNK * block_len
    scale = 1.0 / math.sqrt(HD)
    log2e = 1.0 / math.log(2.0)
    last_block = 2 * group_size - 1
    me = me_ref[0]
    head = me % 2
    pair = me - head
    n_docs = len_ref.shape[1]

    other_copy = pltpu.make_async_copy(other_hbm, other_ref, sems.at[0])
    other_copy.start()

    def place(block):
        early = block < group_size
        slot = jnp.where(early, block, last_block - block)
        return slot, pl.multiple_of(jnp.where(early, 0, block_len), block_len)

    def reach(h):
        first_block = jnp.where(h == 0, pair, last_block - 1 - pair)
        first_pos = first_block * block_len
        end = jnp.int32(0)
        first_start = jnp.int32(0)
        for k in range(n_docs):
            end = end + len_ref[0, k]
            first_start = jnp.where(first_pos >= end, end, first_start)
        low = first_start // block_len
        n_blocks = first_block + 2 - low
        n_chunks = (n_blocks + BLOCKS_PER_CHUNK - 1) // BLOCKS_PER_CHUNK
        return first_block, low, n_blocks, n_chunks

    def load_copy(h, i, first_block, low):
        slot, at = place(jnp.minimum(low + i, first_block + 1))
        into = pl.ds(pl.multiple_of(i * block_len, block_len), block_len)
        return pltpu.make_async_copy(
            kv_ref.at[slot, pl.ds(at, block_len), :],
            windows_ref.at[h, into, :],
            load_sems.at[h, i],
        )

    for h in range(2):
        first_block, low, n_blocks, n_chunks = reach(h)

        def start_load(i, carry, h=h, first_block=first_block, low=low):
            load_copy(h, i, first_block, low).start()
            return carry

        lax.fori_loop(0, n_chunks * BLOCKS_PER_CHUNK, start_load, 0)

    stage_ref[...] = jnp.zeros_like(stage_ref)
    sum_ref[...] = jnp.zeros_like(sum_ref)
    other_copy.wait()

    def query_unit(h, carry):
        first_block, low, n_blocks, n_chunks = reach(h)
        first_pos = first_block * block_len
        win_ref = windows_ref.at[h]
        own_at = pl.multiple_of(jnp.where(h == 0, head, 1 - head) * block_len, block_len)
        partner_at = pl.multiple_of(block_len - own_at, block_len)
        lane = lax.broadcasted_iota(jnp.int32, (1, rows), 1)
        query_pos = first_pos + lane % pair_len
        query_start = jnp.zeros_like(query_pos)
        end = jnp.int32(0)
        for k in range(n_docs):
            end = end + len_ref[0, k]
            query_start = jnp.where(query_pos >= end, end, query_start)

        def wait_load(i, carry):
            load_copy(h, i, first_block, low).wait()
            return carry

        lax.fori_loop(0, n_chunks * BLOCKS_PER_CHUNK, wait_load, 0)

        for t in range(GROUP):
            f = t * HD
            bias = qb_ref[:, lanes(head * HALF_Q + f, HD)]
            own_rows = pl.ds(t * pair_len + own_at, block_len)
            partner_rows = pl.ds(t * pair_len + partner_at, block_len)
            own_lanes = lanes(head * HALF_Q + f, HD)
            q_rows[own_rows, :] = (q_ref[h, :, own_lanes].astype(jnp.float32) + bias).astype(
                jnp.bfloat16
            )
            q_rows[partner_rows, :] = (
                other_ref[0, h, :, f : f + HD].astype(jnp.float32) + bias
            ).astype(jnp.bfloat16)
            d_rows[own_rows, :] = ct_ref[h, :, own_lanes]
            d_rows[partner_rows, :] = other_ref[1, h, :, f : f + HD]

        def window(i):
            return pl.ds(pl.multiple_of(i * chunk, chunk), chunk)

        def score_step(i, top):
            at = window(i)
            s = dot(win_ref[at, :HD], q_rows[...], NT) * (scale * log2e)
            key_pos = (low * block_len + i * chunk) + lax.broadcasted_iota(
                jnp.int32, (chunk, 1), 0
            )
            visible = (key_pos >= query_start) & (key_pos <= query_pos)
            s = jnp.where(visible, s, MASKED)
            p_ref[at, :] = s
            return jnp.maximum(top, jnp.max(s, axis=0, keepdims=True))

        top = lax.fori_loop(0, n_chunks, score_step, jnp.full((1, rows), MASKED, jnp.float32))

        acc_ref[...] = jnp.zeros_like(acc_ref)

        def out_step(i, total):
            at = window(i)
            e = jnp.exp2(p_ref[at, :] - top)
            p_ref[at, :] = e
            acc_ref[...] += dot(win_ref[at, HD:], e.astype(jnp.bfloat16), TN)
            return total + jnp.sum(e, axis=0, keepdims=True)

        total = lax.fori_loop(0, n_chunks, out_step, jnp.zeros((1, rows), jnp.float32))
        inverse = 1.0 / total
        summed = acc_ref[...] * inverse
        delta = jnp.sum(
            summed * jnp.transpose(d_rows[...].astype(jnp.float32)), axis=0, keepdims=True
        )
        row_ref[...] = jnp.transpose(summed)
        for t in range(GROUP):
            f = t * HD
            mine_ref[0, h, :, f : f + HD] = row_ref[
                pl.ds(t * pair_len + own_at, block_len), :
            ].astype(jnp.bfloat16)
            back_ref[0, h, :, f : f + HD] = row_ref[
                pl.ds(t * pair_len + partner_at, block_len), :
            ].astype(jnp.bfloat16)

        acc_ref[...] = jnp.zeros_like(acc_ref)

        def grad_step(i, value_total):
            at = window(i)
            p = p_ref[at, :] * inverse
            dp = dot(win_ref[at, HD:], d_rows[...], NT)
            ds = (p * (dp - delta)).astype(jnp.bfloat16)
            value_part = dot(p.astype(jnp.bfloat16), d_rows[...], NN)
            grad_ref[at, HD:] = value_part
            grad_ref[at, :HD] = dot(ds, q_rows[...], NN) * scale
            acc_ref[...] += dot(win_ref[at, :HD], ds, TN)
            return value_total + jnp.sum(value_part, axis=0, keepdims=True)

        value_total = lax.fori_loop(0, n_chunks, grad_step, jnp.zeros((1, HD), jnp.float32))
        sum_ref[GROUP : GROUP + 1, :] += value_total
        row_ref[...] = jnp.transpose(acc_ref[...] * scale)
        for t in range(GROUP):
            f = t * HD
            mine_ref[1, h, :, f : f + HD] = row_ref[
                pl.ds(t * pair_len + own_at, block_len), :
            ].astype(jnp.bfloat16)
            back_ref[1, h, :, f : f + HD] = row_ref[
                pl.ds(t * pair_len + partner_at, block_len), :
            ].astype(jnp.bfloat16)
            sum_ref[t : t + 1, :] += jnp.sum(
                row_ref[t * pair_len : (t + 1) * pair_len, :], axis=0, keepdims=True
            )

        def store(i, carry):
            slot, at = place(low + i)
            part = grad_ref[pl.ds(pl.multiple_of(i * block_len, block_len), block_len), :]
            into = pl.ds(at, block_len)
            stage_ref[slot, into, :] = (
                stage_ref[slot, into, :].astype(jnp.float32) + part
            ).astype(jnp.bfloat16)
            return carry

        lax.fori_loop(0, n_blocks, store, 0)
        return carry

    lax.fori_loop(0, 2, query_unit, 0)

    sums = sum_ref[...]
    high = sums.astype(jnp.bfloat16).astype(jnp.float32)
    middle = (sums - high).astype(jnp.bfloat16).astype(jnp.float32)
    lowest = sums - high - middle
    pieces = jnp.concatenate(
        [
            jnp.concatenate([high, middle], axis=1),
            jnp.concatenate([lowest, jnp.zeros_like(lowest)], axis=1),
        ],
        axis=0,
    ).astype(jnp.bfloat16)
    for d in range(group_size):
        stage_ref[d, pair_len:, :] = pieces
    copies = [
        pltpu.make_async_copy(back_ref, back_hbm, sems.at[1]),
        pltpu.make_async_copy(stage_ref, gr_ref, sems.at[2]),
        pltpu.make_async_copy(mine_ref, mine_hbm, sems.at[3]),
    ]
    for copy in copies:
        copy.start()
    for copy in copies:
        copy.wait()


def sums_kernel(got_ref, out_ref):
    for g in range(KVH):
        total = got_ref[g].astype(jnp.float32)
        for d in range(g + 2, got_ref.shape[0], 2):
            total += got_ref[d].astype(jnp.float32)
        half = SUM_ROWS // 2
        out_ref[g * half : (g + 1) * half, :] = (
            total[:half, :HD] + total[:half, HD:] + total[half:, :HD]
        )


def finish_kernel(
    group_size, me_ref, got_hbm, mine_ref, theirs_ref, att_ref, qg_ref, kg_ref, vg_ref, got_ref, sems, out_sems
):
    block_len = att_ref.shape[1]
    pair_len = 2 * block_len
    head = me_ref[0] % 2
    part = group_size // GOT_PARTS
    loads = []
    for i in range(GOT_PARTS):
        some = slice(i * part, (i + 1) * part)
        loads.append(
            pltpu.make_async_copy(got_hbm.at[some, :pair_len], got_ref.at[some], sems.at[i])
        )
        loads[i].start()
    copies = []
    for i, ref in enumerate((att_ref, qg_ref)):
        for j, (source, at) in enumerate(((mine_ref, head), (theirs_ref, 1 - head))):
            copies.append(
                pltpu.make_async_copy(
                    source.at[i], ref.at[:, :, lanes(at * HALF_Q, HALF_Q)], out_sems.at[2 * i + j]
                )
            )
            copies[-1].start()
    for load in loads:
        load.wait()
    for h in range(2):
        here = slice(h * block_len, (h + 1) * block_len)
        for g in range(KVH):
            total = got_ref[g, here, :].astype(jnp.float32)
            for d in range(g + 2, group_size, 2):
                total += got_ref[d, here, :].astype(jnp.float32)
            total = total.astype(jnp.bfloat16)
            kg_ref[h, :, g * HD : (g + 1) * HD] = total[:, :HD]
            vg_ref[h, :, g * HD : (g + 1) * HD] = total[:, HD:]
    for copy in copies:
        copy.wait()


def on_device(q_proj, k_proj, v_proj, q_bias, v_bias, cotangent, lengths):
    group_size = lax.axis_size("ctx")
    me = lax.axis_index("ctx").astype(jnp.int32)[None]
    q, ct, k, v = q_proj[0], cotangent[0], k_proj[0], v_proj[0]
    block_len = q.shape[1]
    pair_len = 2 * block_len
    rows = GROUP * pair_len
    most_blocks = MOST // block_len + 2
    window = -(-most_blocks // BLOCKS_PER_CHUNK) * BLOCKS_PER_CHUNK * block_len
    bf16, f32 = jnp.bfloat16, jnp.float32
    halves = jax.ShapeDtypeStruct((2, 2, block_len, HALF_Q), bf16)

    sent, swap = pl.pallas_call(
        functools.partial(send_kernel, group_size),
        out_shape=(jax.ShapeDtypeStruct((group_size, pair_len, SLOT_W), bf16), halves),
        in_specs=[SMEM, VMEM, VMEM, VMEM, HBM, HBM],
        out_specs=(HBM, HBM),
        scratch_shapes=[
            pltpu.VMEM((KVH, pair_len, SLOT_W), bf16),
            pltpu.SemaphoreType.DMA((group_size,)),
            pltpu.SemaphoreType.DMA((2,)),
        ],
        compiler_params=pltpu.CompilerParams(vmem_limit_bytes=VMEM_BYTES),
        name="send",
    )(me, k, v, v_bias[None], q, ct)
    partners = [(i, i ^ 1) for i in range(group_size)]
    other = lax.ppermute(swap, "ctx", partners)
    gathered = lax.all_to_all(sent, "ctx", 0, 0)

    slot_len = pair_len + SUM_ROWS
    slots = (group_size, slot_len, SLOT_W)
    mine, back, parts = pl.pallas_call(
        functools.partial(attention_kernel, group_size),
        out_shape=(halves, halves, jax.ShapeDtypeStruct(slots, bf16)),
        in_specs=[SMEM, SMEM, VMEM, VMEM, HBM, VMEM, HBM],
        out_specs=(HBM, HBM, HBM),
        scratch_shapes=[
            pltpu.VMEM(halves.shape, bf16),
            pltpu.VMEM(halves.shape, bf16),
            pltpu.VMEM(halves.shape, bf16),
            pltpu.VMEM(slots, bf16),
            pltpu.VMEM((2, window, SLOT_W), bf16),
            pltpu.VMEM((rows, HD), bf16),
            pltpu.VMEM((rows, HD), bf16),
            pltpu.VMEM((window, rows), f32),
            pltpu.VMEM((window, SLOT_W), f32),
            pltpu.VMEM((HD, rows), f32),
            pltpu.VMEM((rows, HD), f32),
            pltpu.VMEM((SUM_ROWS // 2, HD), f32),
            pltpu.SemaphoreType.DMA((4,)),
            pltpu.SemaphoreType.DMA((2, window // block_len)),
        ],
        compiler_params=pltpu.CompilerParams(vmem_limit_bytes=VMEM_BYTES),
        cost_estimate=pl.CostEstimate(
            flops=3_000_000_000, bytes_accessed=10_000_000, transcendentals=2_000_000
        ),
        name="attention",
    )(me, lengths, q, ct, other, q_bias[None], gathered)

    theirs = lax.ppermute(back, "ctx", partners)
    got = lax.all_to_all(parts, "ctx", 0, 0)
    sums = pl.pallas_call(
        sums_kernel,
        out_shape=jax.ShapeDtypeStruct((SUM_ROWS, HD), f32),
        grid=(1,),
        in_specs=[
            pl.BlockSpec((group_size, SUM_ROWS, SLOT_W), lambda i: (0, pair_len // SUM_ROWS, 0))
        ],
        out_specs=pl.BlockSpec((SUM_ROWS, HD), lambda i: (0, 0)),
        compiler_params=pltpu.CompilerParams(vmem_limit_bytes=VMEM_BYTES),
        name="sums",
    )(got)
    for axis_step in (1, 2):
        size = lax.axis_size("dp")
        sums = sums + lax.ppermute(sums, "dp", [(i, i ^ axis_step) for i in range(size)])
    wide = jax.ShapeDtypeStruct(q.shape, bf16)
    narrow = jax.ShapeDtypeStruct(k.shape, bf16)
    attended, q_grad, k_grad, v_grad = pl.pallas_call(
        functools.partial(finish_kernel, group_size),
        out_shape=(wide, wide, narrow, narrow),
        in_specs=[SMEM, HBM, HBM, HBM],
        out_specs=(HBM, HBM, VMEM, VMEM),
        scratch_shapes=[
            pltpu.VMEM((group_size, pair_len, SLOT_W), bf16),
            pltpu.SemaphoreType.DMA((GOT_PARTS,)),
            pltpu.SemaphoreType.DMA((4,)),
        ],
        cost_estimate=pl.CostEstimate(flops=1_000_000, bytes_accessed=6_000_000, transcendentals=0),
        compiler_params=pltpu.CompilerParams(vmem_limit_bytes=VMEM_BYTES),
        name="finish",
    )(me, got, mine, theirs)
    by_head = sums.reshape(KVH, SUM_ROWS // 2, HD)
    return (
        attended[None],
        q_grad[None],
        k_grad[None],
        v_grad[None],
        by_head[:, :GROUP].reshape(HQ),
        by_head[:, GROUP].reshape(KW),
    )


def solution(mesh):
    placed = (
        P("dp", None, "ctx", None),
        P("dp", None, "ctx", None),
        P("dp", None, "ctx", None),
        P(),
        P(),
        P("dp", None, "ctx", None),
        P("dp", None),
    )
    return jax.shard_map(
        on_device,
        mesh=mesh,
        in_specs=placed,
        out_specs=(
            P("dp", None, "ctx", None),
            P("dp", None, "ctx", None),
            P("dp", None, "ctx", None),
            P("dp", None, "ctx", None),
            P(),
            P(),
        ),
        check_vma=False,
    )
```

```python
import functools
import math

import jax
import jax.numpy as jnp
from jax import lax
from jax.experimental import pallas as pl
from jax.experimental.pallas import tpu as pltpu
from jax.sharding import PartitionSpec as P

HD = 128
KVH = 2
GROUP = 7
HQ = 1792
KW = 256
MOST = 1024

HALF_Q = GROUP * HD
SLOT_W = 2 * HD
SUM_ROWS = 16
MASKED = -1e30
VMEM_BYTES = 59 * 1024 * 1024
SMALL_BYTES = 16 * 1024 * 1024
BLOCKS_PER_CHUNK = 4

NT = (((1,), (1,)), ((), ()))
NN = (((1,), (0,)), ((), ()))
TN = (((0,), (0,)), ((), ()))

SMEM = pl.BlockSpec(memory_space=pltpu.SMEM)
VMEM = pl.BlockSpec(memory_space=pltpu.VMEM)
ANY = pl.BlockSpec(memory_space=pl.ANY)


def dot(a, b, dims):
    return lax.dot_general(a, b, dims, preferred_element_type=jnp.float32)


def lanes(start, size):
    return pl.ds(pl.multiple_of(start, HD), size)


def swap_kernel(me_ref, q_ref, ct_ref, swap_ref):
    other = 1 - me_ref[0] % 2
    for i, ref in enumerate((q_ref, ct_ref)):
        for h in range(2):
            swap_ref[i, h] = ref[h, :, lanes(other * HALF_Q, HALF_Q)]


def send_kernel(group_size, k_ref, v_ref, vb_ref, send_ref, kv_ref, sem):
    block_len = k_ref.shape[1]
    copies = []
    for g in range(KVH):
        cols = slice(g * HD, (g + 1) * HD)
        for h in range(2):
            here = slice(h * block_len, (h + 1) * block_len)
            kv_ref[g, here, :HD] = k_ref[h, :, cols]
            kv_ref[g, here, HD:] = (
                v_ref[h, :, cols].astype(jnp.float32) + vb_ref[:, cols]
            ).astype(jnp.bfloat16)
        for d in range(g, group_size, KVH):
            copy = pltpu.make_async_copy(kv_ref.at[g], send_ref.at[d], sem.at[d])
            copy.start()
            copies.append(copy)
    for copy in copies:
        copy.wait()


def attention_kernel(
    group_size,
    me_ref,
    len_ref,
    q_ref,
    ct_ref,
    other_hbm,
    qb_ref,
    kv_ref,
    mine_hbm,
    back_hbm,
    gr_ref,
    other_ref,
    mine_ref,
    back_ref,
    stage_ref,
    windows_ref,
    q_rows,
    d_rows,
    p_ref,
    grad_ref,
    acc_ref,
    row_ref,
    sum_ref,
    sems,
    load_sems,
):
    block_len = q_ref.shape[1]
    pair_len = 2 * block_len
    rows = GROUP * pair_len
    chunk = BLOCKS_PER_CHUNK * block_len
    scale = 1.0 / math.sqrt(HD)
    log2e = 1.0 / math.log(2.0)
    last_block = 2 * group_size - 1
    me = me_ref[0]
    head = me % 2
    pair = me - head
    n_docs = len_ref.shape[1]

    other_copy = pltpu.make_async_copy(other_hbm, other_ref, sems.at[0])
    other_copy.start()

    def place(block):
        early = block < group_size
        slot = jnp.where(early, block, last_block - block)
        return slot, pl.multiple_of(jnp.where(early, 0, block_len), block_len)

    def reach(h):
        first_block = jnp.where(h == 0, pair, last_block - 1 - pair)
        first_pos = first_block * block_len
        end = jnp.int32(0)
        first_start = jnp.int32(0)
        for k in range(n_docs):
            end = end + len_ref[0, k]
            first_start = jnp.where(first_pos >= end, end, first_start)
        low = first_start // block_len
        n_blocks = first_block + 2 - low
        n_chunks = (n_blocks + BLOCKS_PER_CHUNK - 1) // BLOCKS_PER_CHUNK
        return first_block, low, n_blocks, n_chunks

    def load_copy(h, i, first_block, low):
        slot, at = place(jnp.minimum(low + i, first_block + 1))
        into = pl.ds(pl.multiple_of(i * block_len, block_len), block_len)
        return pltpu.make_async_copy(
            kv_ref.at[slot, pl.ds(at, block_len), :],
            windows_ref.at[h, into, :],
            load_sems.at[h, i],
        )

    for h in range(2):
        first_block, low, n_blocks, n_chunks = reach(h)

        def start_load(i, carry, h=h, first_block=first_block, low=low):
            load_copy(h, i, first_block, low).start()
            return carry

        lax.fori_loop(0, n_chunks * BLOCKS_PER_CHUNK, start_load, 0)

    stage_ref[...] = jnp.zeros_like(stage_ref)
    sum_ref[...] = jnp.zeros_like(sum_ref)
    other_copy.wait()

    def query_unit(h, carry):
        first_block, low, n_blocks, n_chunks = reach(h)
        first_pos = first_block * block_len
        win_ref = windows_ref.at[h]
        own_at = pl.multiple_of(jnp.where(h == 0, head, 1 - head) * block_len, block_len)
        partner_at = pl.multiple_of(block_len - own_at, block_len)
        lane = lax.broadcasted_iota(jnp.int32, (1, rows), 1)
        query_pos = first_pos + lane % pair_len
        query_start = jnp.zeros_like(query_pos)
        end = jnp.int32(0)
        for k in range(n_docs):
            end = end + len_ref[0, k]
            query_start = jnp.where(query_pos >= end, end, query_start)

        def wait_load(i, carry):
            load_copy(h, i, first_block, low).wait()
            return carry

        lax.fori_loop(0, n_chunks * BLOCKS_PER_CHUNK, wait_load, 0)

        for t in range(GROUP):
            f = t * HD
            bias = qb_ref[:, lanes(head * HALF_Q + f, HD)]
            own_rows = pl.ds(t * pair_len + own_at, block_len)
            partner_rows = pl.ds(t * pair_len + partner_at, block_len)
            own_lanes = lanes(head * HALF_Q + f, HD)
            q_rows[own_rows, :] = (q_ref[h, :, own_lanes].astype(jnp.float32) + bias).astype(
                jnp.bfloat16
            )
            q_rows[partner_rows, :] = (
                other_ref[0, h, :, f : f + HD].astype(jnp.float32) + bias
            ).astype(jnp.bfloat16)
            d_rows[own_rows, :] = ct_ref[h, :, own_lanes]
            d_rows[partner_rows, :] = other_ref[1, h, :, f : f + HD]

        def window(i):
            return pl.ds(pl.multiple_of(i * chunk, chunk), chunk)

        def score_step(i, top):
            at = window(i)
            s = dot(win_ref[at, :HD], q_rows[...], NT) * (scale * log2e)
            key_pos = (low * block_len + i * chunk) + lax.broadcasted_iota(
                jnp.int32, (chunk, 1), 0
            )
            visible = (key_pos >= query_start) & (key_pos <= query_pos)
            s = jnp.where(visible, s, MASKED)
            p_ref[at, :] = s
            return jnp.maximum(top, jnp.max(s, axis=0, keepdims=True))

        top = lax.fori_loop(0, n_chunks, score_step, jnp.full((1, rows), MASKED, jnp.float32))

        acc_ref[...] = jnp.zeros_like(acc_ref)

        def out_step(i, total):
            at = window(i)
            e = jnp.exp2(p_ref[at, :] - top)
            p_ref[at, :] = e
            acc_ref[...] += dot(win_ref[at, HD:], e.astype(jnp.bfloat16), TN)
            return total + jnp.sum(e, axis=0, keepdims=True)

        total = lax.fori_loop(0, n_chunks, out_step, jnp.zeros((1, rows), jnp.float32))
        inverse = 1.0 / total
        summed = acc_ref[...] * inverse
        delta = jnp.sum(
            summed * jnp.transpose(d_rows[...].astype(jnp.float32)), axis=0, keepdims=True
        )
        row_ref[...] = jnp.transpose(summed)
        for t in range(GROUP):
            f = t * HD
            mine_ref[0, h, :, f : f + HD] = row_ref[
                pl.ds(t * pair_len + own_at, block_len), :
            ].astype(jnp.bfloat16)
            back_ref[0, h, :, f : f + HD] = row_ref[
                pl.ds(t * pair_len + partner_at, block_len), :
            ].astype(jnp.bfloat16)

        acc_ref[...] = jnp.zeros_like(acc_ref)

        def grad_step(i, value_total):
            at = window(i)
            p = p_ref[at, :] * inverse
            dp = dot(win_ref[at, HD:], d_rows[...], NT)
            ds = (p * (dp - delta)).astype(jnp.bfloat16)
            value_part = dot(p.astype(jnp.bfloat16), d_rows[...], NN)
            grad_ref[at, HD:] = value_part
            grad_ref[at, :HD] = dot(ds, q_rows[...], NN) * scale
            acc_ref[...] += dot(win_ref[at, :HD], ds, TN)
            return value_total + jnp.sum(value_part, axis=0, keepdims=True)

        value_total = lax.fori_loop(0, n_chunks, grad_step, jnp.zeros((1, HD), jnp.float32))
        sum_ref[GROUP : GROUP + 1, :] += value_total
        row_ref[...] = jnp.transpose(acc_ref[...] * scale)
        for t in range(GROUP):
            f = t * HD
            mine_ref[1, h, :, f : f + HD] = row_ref[
                pl.ds(t * pair_len + own_at, block_len), :
            ].astype(jnp.bfloat16)
            back_ref[1, h, :, f : f + HD] = row_ref[
                pl.ds(t * pair_len + partner_at, block_len), :
            ].astype(jnp.bfloat16)
            sum_ref[t : t + 1, :] += jnp.sum(
                row_ref[t * pair_len : (t + 1) * pair_len, :], axis=0, keepdims=True
            )

        def store(i, carry):
            slot, at = place(low + i)
            part = grad_ref[pl.ds(pl.multiple_of(i * block_len, block_len), block_len), :]
            into = pl.ds(at, block_len)
            stage_ref[slot, into, :] = (
                stage_ref[slot, into, :].astype(jnp.float32) + part
            ).astype(jnp.bfloat16)
            return carry

        lax.fori_loop(0, n_blocks, store, 0)
        return carry

    lax.fori_loop(0, 2, query_unit, 0)

    sums = sum_ref[...]
    high = sums.astype(jnp.bfloat16).astype(jnp.float32)
    middle = (sums - high).astype(jnp.bfloat16).astype(jnp.float32)
    lowest = sums - high - middle
    pieces = jnp.concatenate(
        [
            jnp.concatenate([high, middle], axis=1),
            jnp.concatenate([lowest, jnp.zeros_like(lowest)], axis=1),
        ],
        axis=0,
    ).astype(jnp.bfloat16)
    for d in range(group_size):
        stage_ref[d, pair_len:, :] = pieces
    copies = [
        pltpu.make_async_copy(back_ref, back_hbm, sems.at[1]),
        pltpu.make_async_copy(stage_ref, gr_ref, sems.at[2]),
        pltpu.make_async_copy(mine_ref, mine_hbm, sems.at[3]),
    ]
    for copy in copies:
        copy.start()
    for copy in copies:
        copy.wait()


def join_kernel(me_ref, mine_ref, theirs_ref, att_ref, qg_ref):
    head = me_ref[0] % 2
    for i, ref in enumerate((att_ref, qg_ref)):
        for h in range(2):
            ref[h, :, lanes(head * HALF_Q, HALF_Q)] = mine_ref[i, h]
            ref[h, :, lanes((1 - head) * HALF_Q, HALF_Q)] = theirs_ref[i, h]


def total_kernel(got_ref, kg_ref, vg_ref, sum_ref):
    block_len = kg_ref.shape[1]

    def total_of(g, here):
        total = got_ref[g, here, :].astype(jnp.float32)
        for d in range(g + KVH, got_ref.shape[0], KVH):
            total += got_ref[d, here, :].astype(jnp.float32)
        return total

    for g in range(KVH):
        for h in range(2):
            total = total_of(g, slice(h * block_len, (h + 1) * block_len)).astype(jnp.bfloat16)
            kg_ref[h, :, g * HD : (g + 1) * HD] = total[:, :HD]
            vg_ref[h, :, g * HD : (g + 1) * HD] = total[:, HD:]
        pieces = total_of(g, slice(2 * block_len, 2 * block_len + SUM_ROWS))
        half = SUM_ROWS // 2
        sum_ref[g * half : (g + 1) * half, :] = (
            pieces[:half, :HD] + pieces[:half, HD:] + pieces[half:, :HD]
        )


def on_device(q_proj, k_proj, v_proj, q_bias, v_bias, cotangent, lengths):
    group_size = lax.axis_size("ctx")
    me = lax.axis_index("ctx").astype(jnp.int32)[None]
    q, ct, k, v = q_proj[0], cotangent[0], k_proj[0], v_proj[0]
    block_len = q.shape[1]
    pair_len = 2 * block_len
    rows = GROUP * pair_len
    most_blocks = MOST // block_len + 2
    window = -(-most_blocks // BLOCKS_PER_CHUNK) * BLOCKS_PER_CHUNK * block_len
    bf16, f32 = jnp.bfloat16, jnp.float32
    halves = jax.ShapeDtypeStruct((2, 2, block_len, HALF_Q), bf16)

    swap = pl.pallas_call(
        swap_kernel,
        out_shape=halves,
        in_specs=[SMEM, VMEM, VMEM],
        out_specs=VMEM,
        compiler_params=pltpu.CompilerParams(vmem_limit_bytes=SMALL_BYTES),
        name="swap",
    )(me, q, ct)
    sent = pl.pallas_call(
        functools.partial(send_kernel, group_size),
        out_shape=jax.ShapeDtypeStruct((group_size, pair_len, SLOT_W), bf16),
        in_specs=[VMEM, VMEM, VMEM],
        out_specs=ANY,
        scratch_shapes=[
            pltpu.VMEM((KVH, pair_len, SLOT_W), bf16),
            pltpu.SemaphoreType.DMA((group_size,)),
        ],
        compiler_params=pltpu.CompilerParams(vmem_limit_bytes=VMEM_BYTES),
        name="send",
    )(k, v, v_bias[None])
    partners = [(i, i ^ 1) for i in range(group_size)]
    other = lax.ppermute(swap, "ctx", partners)
    gathered = lax.all_to_all(sent, "ctx", 0, 0)

    slot_len = pair_len + SUM_ROWS
    slots = (group_size, slot_len, SLOT_W)
    mine, back, parts = pl.pallas_call(
        functools.partial(attention_kernel, group_size),
        out_shape=(halves, halves, jax.ShapeDtypeStruct(slots, bf16)),
        in_specs=[SMEM, SMEM, VMEM, VMEM, ANY, VMEM, ANY],
        out_specs=(ANY, ANY, ANY),
        scratch_shapes=[
            pltpu.VMEM(halves.shape, bf16),
            pltpu.VMEM(halves.shape, bf16),
            pltpu.VMEM(halves.shape, bf16),
            pltpu.VMEM(slots, bf16),
            pltpu.VMEM((2, window, SLOT_W), bf16),
            pltpu.VMEM((rows, HD), bf16),
            pltpu.VMEM((rows, HD), bf16),
            pltpu.VMEM((window, rows), f32),
            pltpu.VMEM((window, SLOT_W), f32),
            pltpu.VMEM((HD, rows), f32),
            pltpu.VMEM((rows, HD), f32),
            pltpu.VMEM((SUM_ROWS // 2, HD), f32),
            pltpu.SemaphoreType.DMA((4,)),
            pltpu.SemaphoreType.DMA((2, window // block_len)),
        ],
        compiler_params=pltpu.CompilerParams(vmem_limit_bytes=VMEM_BYTES),
        cost_estimate=pl.CostEstimate(
            flops=3_000_000_000, bytes_accessed=10_000_000, transcendentals=2_000_000
        ),
        name="attention",
    )(me, lengths, q, ct, other, q_bias[None], gathered)

    theirs = lax.ppermute(back, "ctx", partners)
    got = lax.all_to_all(parts, "ctx", 0, 0)
    wide = jax.ShapeDtypeStruct(q.shape, bf16)
    narrow = jax.ShapeDtypeStruct(k.shape, bf16)
    attended, q_grad = pl.pallas_call(
        join_kernel,
        out_shape=(wide, wide),
        in_specs=[SMEM, VMEM, VMEM],
        out_specs=(VMEM, VMEM),
        cost_estimate=pl.CostEstimate(flops=1_000_000, bytes_accessed=4_000_000, transcendentals=0),
        compiler_params=pltpu.CompilerParams(vmem_limit_bytes=SMALL_BYTES),
        name="join",
    )(me, mine, theirs)
    k_grad, v_grad, sums = pl.pallas_call(
        total_kernel,
        out_shape=(narrow, narrow, jax.ShapeDtypeStruct((SUM_ROWS, HD), f32)),
        in_specs=[VMEM],
        out_specs=(VMEM, VMEM, VMEM),
        compiler_params=pltpu.CompilerParams(vmem_limit_bytes=SMALL_BYTES),
        name="total",
    )(got)
    for axis_step in (1, 2):
        size = lax.axis_size("dp")
        sums = sums + lax.ppermute(sums, "dp", [(i, i ^ axis_step) for i in range(size)])
    by_head = sums.reshape(KVH, SUM_ROWS // 2, HD)
    return (
        attended[None],
        q_grad[None],
        k_grad[None],
        v_grad[None],
        by_head[:, :GROUP].reshape(HQ),
        by_head[:, GROUP].reshape(KW),
    )


def solution(mesh):
    placed = (
        P("dp", None, "ctx", None),
        P("dp", None, "ctx", None),
        P("dp", None, "ctx", None),
        P(),
        P(),
        P("dp", None, "ctx", None),
        P("dp", None),
    )
    return jax.shard_map(
        on_device,
        mesh=mesh,
        in_specs=placed,
        out_specs=(
            P("dp", None, "ctx", None),
            P("dp", None, "ctx", None),
            P("dp", None, "ctx", None),
            P("dp", None, "ctx", None),
            P(),
            P(),
        ),
        check_vma=False,
    )
```

```python
import functools
import math

import jax
import jax.numpy as jnp
from jax import lax
from jax.experimental import pallas as pl
from jax.experimental.pallas import tpu as pltpu
from jax.sharding import PartitionSpec as P

HD = 128
KVH = 2
GROUP = 7
HQ = 1792
KW = 256
MOST = 1024

HALF_Q = GROUP * HD
SLOT_W = 2 * HD
SUM_ROWS = 16
MASKED = -1e30
PREP_FLOPS = 5_600_000_000
SWAP_FLOPS = 1_000_000
JOIN_FLOPS = 40_000_000_000
FINISH_FLOPS = 1_000_000
VMEM_BYTES = 59 * 1024 * 1024
SMALL_BYTES = 16 * 1024 * 1024
BLOCKS_PER_CHUNK = 4

NT = (((1,), (1,)), ((), ()))
NN = (((1,), (0,)), ((), ()))
TN = (((0,), (0,)), ((), ()))

SMEM = pl.BlockSpec(memory_space=pltpu.SMEM)
VMEM = pl.BlockSpec(memory_space=pltpu.VMEM)
ANY = pl.BlockSpec(memory_space=pl.ANY)


def dot(a, b, dims):
    return lax.dot_general(a, b, dims, preferred_element_type=jnp.float32)


def lanes(start, size):
    return pl.ds(pl.multiple_of(start, HD), size)


def route(c, d, group_size, reach):
    pair = d - d % 2
    late = (c > pair + 1) & (c <= pair + reach + 1)
    relay = (c < pair - reach) & (c <= group_size - 3 - pair)
    return jnp.where(late, 1, jnp.where(relay, 2, 0))


def blocks_kernel(me_ref, k_hbm, v_hbm, vb_hbm, early_ref, late_ref, near_ref, far_ref, k_ref, v_ref, vb_ref, sems):
    head = me_ref[0] % 2
    pairs = ((k_hbm, k_ref), (v_hbm, v_ref), (vb_hbm, vb_ref))
    loads = [
        pltpu.make_async_copy(source, into, sems.at[i]) for i, (source, into) in enumerate(pairs)
    ]
    for load in loads:
        load.start()
    for load in loads:
        load.wait()
    for h, ref in enumerate((early_ref, late_ref)):
        for g in range(KVH):
            cols = slice(g * HD, (g + 1) * HD)
            ref[g, :, :HD] = k_ref[h, :, cols]
            ref[g, :, HD:] = (v_ref[h, :, cols].astype(jnp.float32) + vb_ref[:, cols]).astype(
                jnp.bfloat16
            )
    near_ref[...] = early_ref[head]
    far_ref[...] = early_ref[1 - head]


def swap_kernel(me_ref, q_hbm, ct_hbm, late_hbm, swap_ref, q_ref, ct_ref, late_ref, sems):
    other = 1 - me_ref[0] % 2
    cols = lanes(other * HALF_Q, HALF_Q)
    pairs = ((q_hbm.at[:, :, cols], q_ref), (ct_hbm.at[:, :, cols], ct_ref), (late_hbm.at[other], late_ref))
    loads = [
        pltpu.make_async_copy(source, into, sems.at[i]) for i, (source, into) in enumerate(pairs)
    ]
    for load in loads:
        load.start()
    for i, ref in enumerate((q_ref, ct_ref)):
        loads[i].wait()
        for h in range(2):
            for t in range(GROUP):
                swap_ref[(2 * i + h) * GROUP + t] = ref[h, :, t * HD : (t + 1) * HD]
    loads[2].wait()
    swap_ref[4 * GROUP] = late_ref[:, :HD]
    swap_ref[4 * GROUP + 1] = late_ref[:, HD:]


def prepare_kernel(
    me_ref, q_ref, ct_ref, other_ref, qb_ref, q_rows, d_rows
):
    block_len = q_ref.shape[1]
    pair_len = 2 * block_len
    head = me_ref[0] % 2
    for h in range(2):
        own_at = pl.multiple_of((head if h == 0 else 1 - head) * block_len, block_len)
        partner_at = pl.multiple_of(block_len - own_at, block_len)
        for t in range(GROUP):
            own_lanes = lanes(head * HALF_Q + t * HD, HD)
            bias = qb_ref[:, own_lanes]
            own_rows = pl.ds(t * pair_len + own_at, block_len)
            partner_rows = pl.ds(t * pair_len + partner_at, block_len)
            q_rows[h, own_rows, :] = (q_ref[h, :, own_lanes].astype(jnp.float32) + bias).astype(
                jnp.bfloat16
            )
            q_rows[h, partner_rows, :] = (
                other_ref[h * GROUP + t].astype(jnp.float32) + bias
            ).astype(jnp.bfloat16)
            d_rows[h, own_rows, :] = ct_ref[h, :, own_lanes]
            d_rows[h, partner_rows, :] = other_ref[(2 + h) * GROUP + t]


def send_kernel(
    group_size, reach, me_ref, early_hbm, late_hbm, relay_hbm, near_hbm, far_hbm, send_ref, all_ref, sem, load_sems
):
    me = me_ref[0]
    loads = [
        pltpu.make_async_copy(source, all_ref.at[i], load_sems.at[i])
        for i, source in enumerate((early_hbm, late_hbm, relay_hbm))
    ]
    for load in loads:
        load.start()
    for load in loads:
        load.wait()
    copies = []
    for d in range(group_size):
        kind = route(me, jnp.int32(d), group_size, reach)
        copy = pltpu.make_async_copy(all_ref.at[kind, d % KVH], send_ref.at[d], sem.at[d])
        copy.start()
        copies.append(copy)
    for copy in copies:
        copy.wait()


def attention_kernel(
    group_size,
    reach,
    me_ref,
    len_ref,
    q_hbm,
    d_hbm,
    other_hbm,
    kv_hbm,
    late_hbm,
    near_hbm,
    far_hbm,
    mine_hbm,
    back_hbm,
    parts_hbm,
    own_hbm,
    near_grad_hbm,
    far_grad_hbm,
    other_ref,
    mine_ref,
    back_ref,
    all_ref,
    stage_ref,
    win_ref,
    q_both,
    d_both,
    p_ref,
    grad_ref,
    acc_ref,
    row_ref,
    sum_ref,
    in_sems,
    out_sems,
):
    block_len = mine_ref.shape[1]
    pair_len = 2 * block_len
    rows = GROUP * pair_len
    chunk = BLOCKS_PER_CHUNK * block_len
    scale = 1.0 / math.sqrt(HD)
    log2e = 1.0 / math.log(2.0)
    last_block = 2 * group_size - 1
    me = me_ref[0]
    head = me % 2
    pair = me - head
    n_docs = len_ref.shape[1]
    own_late, other_late, near, far = range(group_size, group_size + 4)

    loads = [
        pltpu.make_async_copy(source, into, in_sems.at[i])
        for i, (source, into) in enumerate(
            (
                (other_hbm.at[4 * GROUP :], other_ref),
                (q_hbm, q_both),
                (d_hbm, d_both),
                (kv_hbm, all_ref.at[:group_size]),
                (late_hbm.at[head], all_ref.at[own_late]),
                (near_hbm, all_ref.at[near]),
                (far_hbm, all_ref.at[far]),
            )
        )
    ]
    for load in loads:
        load.start()

    def place(block):
        lowest_late = last_block - 1 - pair - reach
        doubled = jnp.where(
            group_size - 1 - block < pair - reach,
            group_size - 1 - block,
            jnp.where(block == lowest_late + head, near, far),
        )
        early = jnp.where(block <= pair + 1, block, doubled)
        c = last_block - block
        late = jnp.where(c == me, own_late, jnp.where(c == pair + 1 - head, other_late, c))
        return jnp.where(block < group_size, early, late)

    stage_ref[...] = jnp.zeros_like(stage_ref)
    sum_ref[...] = jnp.zeros_like(sum_ref)
    for load in loads:
        load.wait()
    all_ref[other_late, :, :HD] = other_ref[0]
    all_ref[other_late, :, HD:] = other_ref[1]

    def query_unit(h, carry):
        first_block = jnp.where(h == 0, pair, last_block - 1 - pair)
        first_pos = first_block * block_len
        own_at = pl.multiple_of(jnp.where(h == 0, head, 1 - head) * block_len, block_len)
        partner_at = pl.multiple_of(block_len - own_at, block_len)
        lane = lax.broadcasted_iota(jnp.int32, (1, rows), 1)
        query_pos = first_pos + lane % pair_len
        query_start = jnp.zeros_like(query_pos)
        end = jnp.int32(0)
        first_start = jnp.int32(0)
        for k in range(n_docs):
            end = end + len_ref[0, k]
            query_start = jnp.where(query_pos >= end, end, query_start)
            first_start = jnp.where(first_pos >= end, end, first_start)
        low = first_start // block_len
        n_blocks = first_block + 2 - low
        n_chunks = (n_blocks + BLOCKS_PER_CHUNK - 1) // BLOCKS_PER_CHUNK

        def load(i, carry):
            win_ref[pl.ds(pl.multiple_of(i * block_len, block_len), block_len), :] = all_ref[
                place(jnp.minimum(low + i, first_block + 1))
            ]
            return carry

        lax.fori_loop(0, n_chunks * BLOCKS_PER_CHUNK, load, 0)

        q_rows, d_rows = q_both.at[h], d_both.at[h]

        def window(i):
            return pl.ds(pl.multiple_of(i * chunk, chunk), chunk)

        def score_step(i, top):
            at = window(i)
            s = dot(win_ref[at, :HD], q_rows[...], NT) * (scale * log2e)
            key_pos = (low * block_len + i * chunk) + lax.broadcasted_iota(
                jnp.int32, (chunk, 1), 0
            )
            visible = (key_pos >= query_start) & (key_pos <= query_pos)
            s = jnp.where(visible, s, MASKED)
            p_ref[at, :] = s
            return jnp.maximum(top, jnp.max(s, axis=0, keepdims=True))

        top = lax.fori_loop(0, n_chunks, score_step, jnp.full((1, rows), MASKED, jnp.float32))

        acc_ref[...] = jnp.zeros_like(acc_ref)

        def out_step(i, total):
            at = window(i)
            e = jnp.exp2(p_ref[at, :] - top)
            p_ref[at, :] = e
            acc_ref[...] += dot(win_ref[at, HD:], e.astype(jnp.bfloat16), TN)
            return total + jnp.sum(e, axis=0, keepdims=True)

        total = lax.fori_loop(0, n_chunks, out_step, jnp.zeros((1, rows), jnp.float32))
        inverse = 1.0 / total
        summed = acc_ref[...] * inverse
        delta = jnp.sum(
            summed * jnp.transpose(d_rows[...].astype(jnp.float32)), axis=0, keepdims=True
        )
        row_ref[...] = jnp.transpose(summed)
        for t in range(GROUP):
            mine_ref[h * GROUP + t] = row_ref[
                pl.ds(t * pair_len + own_at, block_len), :
            ].astype(jnp.bfloat16)
            back_ref[h * GROUP + t] = row_ref[
                pl.ds(t * pair_len + partner_at, block_len), :
            ].astype(jnp.bfloat16)

        acc_ref[...] = jnp.zeros_like(acc_ref)

        def grad_step(i, value_total):
            at = window(i)
            p = p_ref[at, :] * inverse
            dp = dot(win_ref[at, HD:], d_rows[...], NT)
            ds = (p * (dp - delta)).astype(jnp.bfloat16)
            value_part = dot(p.astype(jnp.bfloat16), d_rows[...], NN)
            grad_ref[at, HD:] = value_part
            grad_ref[at, :HD] = dot(ds, q_rows[...], NN) * scale
            acc_ref[...] += dot(win_ref[at, :HD], ds, TN)
            return value_total + jnp.sum(value_part, axis=0, keepdims=True)

        value_total = lax.fori_loop(0, n_chunks, grad_step, jnp.zeros((1, HD), jnp.float32))
        sum_ref[GROUP : GROUP + 1, :] += value_total
        row_ref[...] = jnp.transpose(acc_ref[...] * scale)
        for t in range(GROUP):
            mine_ref[(2 + h) * GROUP + t] = row_ref[
                pl.ds(t * pair_len + own_at, block_len), :
            ].astype(jnp.bfloat16)
            back_ref[(2 + h) * GROUP + t] = row_ref[
                pl.ds(t * pair_len + partner_at, block_len), :
            ].astype(jnp.bfloat16)
            sum_ref[t : t + 1, :] += jnp.sum(
                row_ref[t * pair_len : (t + 1) * pair_len, :], axis=0, keepdims=True
            )

        def store(i, carry):
            slot = place(low + i)
            part = grad_ref[pl.ds(pl.multiple_of(i * block_len, block_len), block_len), :]
            stage_ref[slot, :block_len, :] = (
                stage_ref[slot, :block_len, :].astype(jnp.float32) + part
            ).astype(jnp.bfloat16)
            return carry

        lax.fori_loop(0, n_blocks, store, 0)
        return carry

    lax.fori_loop(0, 2, query_unit, 0)

    sums = sum_ref[...]
    high = sums.astype(jnp.bfloat16).astype(jnp.float32)
    middle = (sums - high).astype(jnp.bfloat16).astype(jnp.float32)
    lowest = sums - high - middle
    pieces = jnp.concatenate(
        [
            jnp.concatenate([high, middle], axis=1),
            jnp.concatenate([lowest, jnp.zeros_like(lowest)], axis=1),
        ],
        axis=0,
    ).astype(jnp.bfloat16)
    for d in range(group_size):
        stage_ref[d, block_len:, :] = pieces
    back_ref[4 * GROUP] = stage_ref[other_late, :block_len, :HD]
    back_ref[4 * GROUP + 1] = stage_ref[other_late, :block_len, HD:]
    stores = [
        pltpu.make_async_copy(source, into, out_sems.at[i])
        for i, (source, into) in enumerate(
            (
                (back_ref, back_hbm),
                (stage_ref.at[near, :block_len], near_grad_hbm),
                (stage_ref.at[far, :block_len], far_grad_hbm),
                (stage_ref.at[:group_size], parts_hbm),
                (mine_ref, mine_hbm),
                (stage_ref.at[own_late, :block_len], own_hbm),
            )
        )
    ]
    for store in stores:
        store.start()
    for store in stores:
        store.wait()


def join_kernel(me_ref, mine_ref, theirs_ref, near_hbm, far_hbm, att_ref, qg_ref):
    head = me_ref[0] % 2
    for i, ref in enumerate((att_ref, qg_ref)):
        for h in range(2):
            for t in range(GROUP):
                tile = (2 * i + h) * GROUP + t
                ref[h, :, lanes(head * HALF_Q + t * HD, HD)] = mine_ref[tile]
                ref[h, :, lanes((1 - head) * HALF_Q + t * HD, HD)] = theirs_ref[tile]


def total_kernel(
    group_size,
    reach,
    me_ref,
    got_ref,
    near_ref,
    far_ref,
    own_ref,
    theirs_ref,
    joined_hbm,
    relay_ref,
    total_ref,
    sum_ref,
    acc_ref,
):
    block_len = total_ref.shape[2]
    me = me_ref[0]
    head = me % 2
    half = SUM_ROWS // 2
    acc_ref[2] = jnp.zeros_like(acc_ref[2])
    acc_ref[0, head] = near_ref[...].astype(jnp.float32)
    acc_ref[0, 1 - head] = far_ref[...].astype(jnp.float32)
    acc_ref[1, head] = own_ref[...].astype(jnp.float32)
    acc_ref[1, 1 - head, :, :HD] = theirs_ref[4 * GROUP].astype(jnp.float32)
    acc_ref[1, 1 - head, :, HD:] = theirs_ref[4 * GROUP + 1].astype(jnp.float32)
    for d in range(group_size):
        kind = route(me, jnp.int32(d), group_size, reach)
        acc_ref[kind, d % KVH] += got_ref[d, :block_len, :].astype(jnp.float32)
    total_ref[...] = acc_ref[:2]
    relay_ref[...] = acc_ref[2].astype(jnp.bfloat16)
    for g in range(KVH):
        pieces = got_ref[g, block_len:, :].astype(jnp.float32)
        for d in range(g + KVH, group_size, KVH):
            pieces += got_ref[d, block_len:, :].astype(jnp.float32)
        sum_ref[g * half : (g + 1) * half, :] = (
            pieces[:half, :HD] + pieces[:half, HD:] + pieces[half:, :HD]
        )


def finish_kernel(total_ref, relay_ref, kg_ref, vg_ref):
    for g in range(KVH):
        cols = slice(g * HD, (g + 1) * HD)
        early = total_ref[0, g] + relay_ref[g].astype(jnp.float32)
        for h, total in enumerate((early, total_ref[1, g])):
            total = total.astype(jnp.bfloat16)
            kg_ref[h, :, cols] = total[:, :HD]
            vg_ref[h, :, cols] = total[:, HD:]


def bias_kernel(a_ref, b_ref, finished_hbm, q_sum_ref, v_sum_ref):
    total = a_ref[...] + b_ref[...]
    half = SUM_ROWS // 2
    for g in range(KVH):
        for t in range(GROUP):
            at = (g * GROUP + t) * HD
            q_sum_ref[:, at : at + HD] = total[g * half + t : g * half + t + 1]
        v_sum_ref[:, g * HD : (g + 1) * HD] = total[g * half + GROUP : (g + 1) * half]


def on_device(q_proj, k_proj, v_proj, q_bias, v_bias, cotangent, lengths):
    group_size = lax.axis_size("ctx")
    me = lax.axis_index("ctx").astype(jnp.int32)[None]
    q, ct, k, v = q_proj[0], cotangent[0], k_proj[0], v_proj[0]
    block_len = q.shape[1]
    reach = MOST // block_len
    rows = GROUP * 2 * block_len
    window = -(-(reach + 2) // BLOCKS_PER_CHUNK) * BLOCKS_PER_CHUNK * block_len
    bf16, f32 = jnp.bfloat16, jnp.float32
    tiles = jax.ShapeDtypeStruct((4 * GROUP, block_len, HD), bf16)
    more_tiles = jax.ShapeDtypeStruct((4 * GROUP + 2, block_len, HD), bf16)
    block = jax.ShapeDtypeStruct((block_len, SLOT_W), bf16)
    by_head = jax.ShapeDtypeStruct((KVH, block_len, SLOT_W), bf16)
    small = pltpu.CompilerParams(vmem_limit_bytes=SMALL_BYTES)
    large = pltpu.CompilerParams(vmem_limit_bytes=VMEM_BYTES)

    partners = [(i, i ^ 1) for i in range(group_size)]
    relays = [(i, group_size - 1 - i) for i in range(group_size - group_size // 4, group_size)]
    to_near, to_far = [], []
    for p in range(group_size // 2, group_size - group_size // 4, 2):
        lowest_late = 2 * group_size - 2 - p - reach
        for g in range(2):
            to_near.append((lowest_late + g, p + g))
            to_far.append((lowest_late + 1 - g, p + g))

    half_cols = (2, block_len, HALF_Q)
    row_pairs = jax.ShapeDtypeStruct((2, rows, HD), bf16)
    early, late, near, far = pl.pallas_call(
        blocks_kernel,
        out_shape=(by_head, by_head, block, block),
        in_specs=[SMEM] + [ANY] * 3,
        out_specs=(VMEM,) * 4,
        scratch_shapes=[
            pltpu.VMEM(k.shape, bf16),
            pltpu.VMEM(k.shape, bf16),
            pltpu.VMEM((1, KW), f32),
            pltpu.SemaphoreType.DMA((3,)),
        ],
        compiler_params=large,
        name="blocks",
    )(me, k, v, v_bias[None])
    relayed = lax.ppermute(early, "ctx", relays)
    near = lax.ppermute(near, "ctx", to_near)
    far = lax.ppermute(far, "ctx", to_far)
    swap = pl.pallas_call(
        swap_kernel,
        out_shape=more_tiles,
        in_specs=[SMEM, ANY, ANY, ANY],
        out_specs=VMEM,
        scratch_shapes=[
            pltpu.VMEM(half_cols, bf16),
            pltpu.VMEM(half_cols, bf16),
            pltpu.VMEM(block.shape, bf16),
            pltpu.SemaphoreType.DMA((3,)),
        ],
        compiler_params=large,
        cost_estimate=pl.CostEstimate(
            flops=SWAP_FLOPS, bytes_accessed=2_000_000, transcendentals=0
        ),
        name="swap",
    )(me, q, ct, late)
    other = lax.ppermute(swap, "ctx", partners)
    sent = pl.pallas_call(
        functools.partial(send_kernel, group_size, reach),
        out_shape=jax.ShapeDtypeStruct((group_size, block_len, SLOT_W), bf16),
        in_specs=[SMEM] + [ANY] * 5,
        out_specs=ANY,
        scratch_shapes=[
            pltpu.VMEM((3, KVH, block_len, SLOT_W), bf16),
            pltpu.SemaphoreType.DMA((group_size,)),
            pltpu.SemaphoreType.DMA((3,)),
        ],
        compiler_params=large,
        name="send",
    )(me, early, late, relayed, near, far)
    gathered = lax.all_to_all(sent, "ctx", 0, 0)
    q_rows, d_rows = pl.pallas_call(
        prepare_kernel,
        out_shape=(row_pairs, row_pairs),
        in_specs=[SMEM] + [VMEM] * 4,
        out_specs=(VMEM, VMEM),
        cost_estimate=pl.CostEstimate(
            flops=PREP_FLOPS, bytes_accessed=4_000_000, transcendentals=0
        ),
        compiler_params=small,
        name="prepare",
    )(me, q, ct, other, q_bias[None])

    slot_len = block_len + SUM_ROWS
    mine, back, parts, own, near_grad, far_grad = pl.pallas_call(
        functools.partial(attention_kernel, group_size, reach),
        out_shape=(
            tiles,
            more_tiles,
            jax.ShapeDtypeStruct((group_size, slot_len, SLOT_W), bf16),
            block,
            block,
            block,
        ),
        in_specs=[SMEM, SMEM] + [ANY] * 7,
        out_specs=(ANY,) * 6,
        scratch_shapes=[
            pltpu.VMEM((2, block_len, HD), bf16),
            pltpu.VMEM(tiles.shape, bf16),
            pltpu.VMEM(more_tiles.shape, bf16),
            pltpu.VMEM((group_size + 4, block_len, SLOT_W), bf16),
            pltpu.VMEM((group_size + 4, slot_len, SLOT_W), bf16),
            pltpu.VMEM((window, SLOT_W), bf16),
            pltpu.VMEM(row_pairs.shape, bf16),
            pltpu.VMEM(row_pairs.shape, bf16),
            pltpu.VMEM((window, rows), f32),
            pltpu.VMEM((window, SLOT_W), f32),
            pltpu.VMEM((HD, rows), f32),
            pltpu.VMEM((rows, HD), f32),
            pltpu.VMEM((SUM_ROWS // 2, HD), f32),
            pltpu.SemaphoreType.DMA((7,)),
            pltpu.SemaphoreType.DMA((6,)),
        ],
        compiler_params=large,
        cost_estimate=pl.CostEstimate(
            flops=3_000_000_000, bytes_accessed=10_000_000, transcendentals=2_000_000
        ),
        name="attention",
    )(me, lengths, q_rows, d_rows, other, gathered, late, near, far)

    def back_along(pairs):
        return [(target, source) for source, target in pairs]

    theirs = lax.ppermute(back, "ctx", partners)
    near_grad = lax.ppermute(near_grad, "ctx", back_along(to_near))
    far_grad = lax.ppermute(far_grad, "ctx", back_along(to_far))
    got = lax.all_to_all(parts, "ctx", 0, 0)
    wide = jax.ShapeDtypeStruct(q.shape, bf16)
    narrow = jax.ShapeDtypeStruct(k.shape, bf16)
    attended, q_grad = pl.pallas_call(
        join_kernel,
        out_shape=(wide, wide),
        in_specs=[SMEM, VMEM, VMEM, ANY, ANY],
        out_specs=(VMEM, VMEM),
        cost_estimate=pl.CostEstimate(
            flops=JOIN_FLOPS, bytes_accessed=4_000_000, transcendentals=0
        ),
        compiler_params=small,
        name="join",
    )(me, mine, theirs, near_grad, far_grad)
    relay_total, total, sums = pl.pallas_call(
        functools.partial(total_kernel, group_size, reach),
        out_shape=(
            by_head,
            jax.ShapeDtypeStruct((2, KVH, block_len, SLOT_W), f32),
            jax.ShapeDtypeStruct((SUM_ROWS, HD), f32),
        ),
        in_specs=[SMEM] + [VMEM] * 5 + [ANY],
        out_specs=(VMEM, VMEM, VMEM),
        scratch_shapes=[pltpu.VMEM((3, KVH, block_len, SLOT_W), f32)],
        compiler_params=small,
        name="total",
    )(me, got, near_grad, far_grad, own, theirs, q_grad)
    relay_grad = lax.ppermute(relay_total, "ctx", back_along(relays))
    dp_size = lax.axis_size("dp")
    sums = sums + lax.ppermute(sums, "dp", [(i, i ^ 1) for i in range(dp_size)])
    other_sums = lax.ppermute(sums, "dp", [(i, i ^ 2) for i in range(dp_size)])
    k_grad, v_grad = pl.pallas_call(
        finish_kernel,
        out_shape=(narrow, narrow),
        in_specs=[VMEM, VMEM],
        out_specs=(VMEM, VMEM),
        cost_estimate=pl.CostEstimate(
            flops=FINISH_FLOPS, bytes_accessed=1_000_000, transcendentals=0
        ),
        compiler_params=small,
        name="finish",
    )(total, relay_grad)
    q_sum, v_sum = pl.pallas_call(
        bias_kernel,
        out_shape=(jax.ShapeDtypeStruct((1, HQ), f32), jax.ShapeDtypeStruct((1, KW), f32)),
        in_specs=[VMEM, VMEM, ANY],
        out_specs=(VMEM, VMEM),
        compiler_params=small,
        name="bias",
    )(sums, other_sums, k_grad)
    return (
        attended[None],
        q_grad[None],
        k_grad[None],
        v_grad[None],
        q_sum.reshape(HQ),
        v_sum.reshape(KW),
    )


def solution(mesh):
    placed = (
        P("dp", None, "ctx", None),
        P("dp", None, "ctx", None),
        P("dp", None, "ctx", None),
        P(),
        P(),
        P("dp", None, "ctx", None),
        P("dp", None),
    )
    return jax.shard_map(
        on_device,
        mesh=mesh,
        in_specs=placed,
        out_specs=(
            P("dp", None, "ctx", None),
            P("dp", None, "ctx", None),
            P("dp", None, "ctx", None),
            P("dp", None, "ctx", None),
            P(),
            P(),
        ),
        check_vma=False,
    )
```

```python
import functools
import math

import jax
import jax.numpy as jnp
from jax import lax
from jax.experimental import pallas as pl
from jax.experimental.pallas import tpu as pltpu
from jax.sharding import PartitionSpec as P

HD = 128
KVH = 2
GROUP = 7
HQ = 1792
KW = 256
MOST = 1024

HALF_Q = GROUP * HD
SLOT_W = 2 * HD
SUM_ROWS = 16
MASKED = -1e30
PREP_FLOPS = 5_600_000_000
SWAP_FLOPS = 1_000_000
JOIN_FLOPS = 40_000_000_000
FINISH_FLOPS = 1_000_000
BIAS_FLOPS = 10_000_000_000
VMEM_BYTES = 59 * 1024 * 1024
SMALL_BYTES = 16 * 1024 * 1024
BLOCKS_PER_CHUNK = 4

NT = (((1,), (1,)), ((), ()))
NN = (((1,), (0,)), ((), ()))
TN = (((0,), (0,)), ((), ()))

SMEM = pl.BlockSpec(memory_space=pltpu.SMEM)
VMEM = pl.BlockSpec(memory_space=pltpu.VMEM)
ANY = pl.BlockSpec(memory_space=pl.ANY)


def dot(a, b, dims):
    return lax.dot_general(a, b, dims, preferred_element_type=jnp.float32)


def lanes(start, size):
    return pl.ds(pl.multiple_of(start, HD), size)


def route(c, d, group_size, reach):
    pair = d - d % 2
    late = (c > pair + 1) & (c <= pair + reach + 1)
    relay = (c < pair - reach) & (c <= group_size - 3 - pair)
    return jnp.where(late, 1, jnp.where(relay, 2, 0))


def blocks_kernel(me_ref, k_hbm, v_hbm, vb_hbm, early_ref, late_ref, near_ref, far_ref, k_ref, v_ref, vb_ref, sems):
    head = me_ref[0] % 2
    pairs = ((k_hbm, k_ref), (v_hbm, v_ref), (vb_hbm, vb_ref))
    loads = [
        pltpu.make_async_copy(source, into, sems.at[i]) for i, (source, into) in enumerate(pairs)
    ]
    for load in loads:
        load.start()
    for load in loads:
        load.wait()
    for h, ref in enumerate((early_ref, late_ref)):
        for g in range(KVH):
            cols = slice(g * HD, (g + 1) * HD)
            ref[g, :, :HD] = k_ref[h, :, cols]
            ref[g, :, HD:] = (v_ref[h, :, cols].astype(jnp.float32) + vb_ref[:, cols]).astype(
                jnp.bfloat16
            )
    near_ref[...] = early_ref[head]
    far_ref[...] = early_ref[1 - head]


def swap_kernel(me_ref, q_hbm, ct_hbm, late_hbm, swap_ref, q_ref, ct_ref, late_ref, sems):
    other = 1 - me_ref[0] % 2
    cols = lanes(other * HALF_Q, HALF_Q)
    pairs = ((q_hbm.at[:, :, cols], q_ref), (ct_hbm.at[:, :, cols], ct_ref), (late_hbm.at[other], late_ref))
    loads = [
        pltpu.make_async_copy(source, into, sems.at[i]) for i, (source, into) in enumerate(pairs)
    ]
    for load in loads:
        load.start()
    for i, ref in enumerate((q_ref, ct_ref)):
        loads[i].wait()
        for h in range(2):
            for t in range(GROUP):
                swap_ref[(2 * i + h) * GROUP + t] = ref[h, :, t * HD : (t + 1) * HD]
    loads[2].wait()
    swap_ref[4 * GROUP] = late_ref[:, :HD]
    swap_ref[4 * GROUP + 1] = late_ref[:, HD:]


def prepare_kernel(
    me_ref, q_ref, ct_ref, other_ref, qb_ref, q_rows, d_rows, d_cols
):
    block_len = q_ref.shape[1]
    pair_len = 2 * block_len
    head = me_ref[0] % 2
    for h in range(2):
        own_at = pl.multiple_of((head if h == 0 else 1 - head) * block_len, block_len)
        partner_at = pl.multiple_of(block_len - own_at, block_len)
        for t in range(GROUP):
            own_lanes = lanes(head * HALF_Q + t * HD, HD)
            bias = qb_ref[:, own_lanes]
            own_rows = pl.ds(t * pair_len + own_at, block_len)
            partner_rows = pl.ds(t * pair_len + partner_at, block_len)
            q_rows[h, own_rows, :] = (q_ref[h, :, own_lanes].astype(jnp.float32) + bias).astype(
                jnp.bfloat16
            )
            q_rows[h, partner_rows, :] = (
                other_ref[h * GROUP + t].astype(jnp.float32) + bias
            ).astype(jnp.bfloat16)
            d_rows[h, own_rows, :] = ct_ref[h, :, own_lanes]
            d_rows[h, partner_rows, :] = other_ref[(2 + h) * GROUP + t]
        d_cols[h] = jnp.transpose(d_rows[h].astype(jnp.float32)).astype(jnp.bfloat16)


def send_kernel(
    group_size, reach, me_ref, early_ref, late_ref, relay_ref, near_hbm, far_hbm, send_ref, all_ref, sem
):
    me = me_ref[0]
    all_ref[0] = early_ref[...]
    all_ref[1] = late_ref[...]
    all_ref[2] = relay_ref[...]
    copies = []
    for d in range(group_size):
        kind = route(me, jnp.int32(d), group_size, reach)
        copy = pltpu.make_async_copy(all_ref.at[kind, d % KVH], send_ref.at[d], sem.at[d])
        copy.start()
        copies.append(copy)
    for copy in copies:
        copy.wait()


def attention_kernel(
    group_size,
    reach,
    me_ref,
    len_ref,
    q_hbm,
    d_hbm,
    dt_hbm,
    other_hbm,
    kv_hbm,
    late_hbm,
    near_hbm,
    far_hbm,
    mine_hbm,
    back_hbm,
    parts_hbm,
    near_grad_hbm,
    far_grad_hbm,
    other_ref,
    mine_ref,
    back_ref,
    all_ref,
    stage_ref,
    win_ref,
    q_both,
    d_both,
    dt_both,
    p_ref,
    grad_ref,
    acc_ref,
    row_ref,
    sum_ref,
    in_sems,
    out_sems,
):
    block_len = mine_ref.shape[1]
    pair_len = 2 * block_len
    rows = GROUP * pair_len
    chunk = BLOCKS_PER_CHUNK * block_len
    scale = 1.0 / math.sqrt(HD)
    log2e = 1.0 / math.log(2.0)
    last_block = 2 * group_size - 1
    me = me_ref[0]
    head = me % 2
    pair = me - head
    n_docs = len_ref.shape[1]
    own_late, other_late, near, far = range(group_size, group_size + 4)

    loads = [
        pltpu.make_async_copy(source, into, in_sems.at[i])
        for i, (source, into) in enumerate(
            (
                (other_hbm.at[4 * GROUP :], other_ref),
                (q_hbm, q_both),
                (d_hbm, d_both),
                (dt_hbm, dt_both),
                (kv_hbm, all_ref.at[:group_size]),
                (late_hbm.at[head], all_ref.at[own_late]),
                (near_hbm, all_ref.at[near]),
                (far_hbm, all_ref.at[far]),
            )
        )
    ]
    for load in loads:
        load.start()

    def place(block):
        lowest_late = last_block - 1 - pair - reach
        doubled = jnp.where(
            group_size - 1 - block < pair - reach,
            group_size - 1 - block,
            jnp.where(block == lowest_late + head, near, far),
        )
        early = jnp.where(block <= pair + 1, block, doubled)
        c = last_block - block
        late = jnp.where(c == me, own_late, jnp.where(c == pair + 1 - head, other_late, c))
        return jnp.where(block < group_size, early, late)

    stage_ref[...] = jnp.zeros_like(stage_ref)
    sum_ref[...] = jnp.zeros_like(sum_ref)
    for load in loads:
        load.wait()
    all_ref[other_late, :, :HD] = other_ref[0]
    all_ref[other_late, :, HD:] = other_ref[1]

    def query_unit(h, carry):
        first_block = jnp.where(h == 0, pair, last_block - 1 - pair)
        first_pos = first_block * block_len
        own_at = pl.multiple_of(jnp.where(h == 0, head, 1 - head) * block_len, block_len)
        partner_at = pl.multiple_of(block_len - own_at, block_len)
        lane = lax.broadcasted_iota(jnp.int32, (1, rows), 1)
        query_pos = first_pos + lane % pair_len
        query_start = jnp.zeros_like(query_pos)
        end = jnp.int32(0)
        first_start = jnp.int32(0)
        for k in range(n_docs):
            end = end + len_ref[0, k]
            query_start = jnp.where(query_pos >= end, end, query_start)
            first_start = jnp.where(first_pos >= end, end, first_start)
        low = first_start // block_len
        n_blocks = first_block + 2 - low
        n_chunks = (n_blocks + BLOCKS_PER_CHUNK - 1) // BLOCKS_PER_CHUNK

        def load(i, carry):
            win_ref[pl.ds(pl.multiple_of(i * block_len, block_len), block_len), :] = all_ref[
                place(jnp.minimum(low + i, first_block + 1))
            ]
            return carry

        lax.fori_loop(0, n_chunks * BLOCKS_PER_CHUNK, load, 0)

        q_rows, d_rows = q_both.at[h], d_both.at[h]

        def window(i):
            return pl.ds(pl.multiple_of(i * chunk, chunk), chunk)

        def score_step(i, top):
            at = window(i)
            s = dot(win_ref[at, :HD], q_rows[...], NT) * (scale * log2e)
            key_pos = (low * block_len + i * chunk) + lax.broadcasted_iota(
                jnp.int32, (chunk, 1), 0
            )
            visible = (key_pos >= query_start) & (key_pos <= query_pos)
            s = jnp.where(visible, s, MASKED)
            p_ref[at, :] = s
            return jnp.maximum(top, jnp.max(s, axis=0, keepdims=True))

        top = lax.fori_loop(0, n_chunks, score_step, jnp.full((1, rows), MASKED, jnp.float32))

        acc_ref[...] = jnp.zeros_like(acc_ref)

        def out_step(i, total):
            at = window(i)
            e = jnp.exp2(p_ref[at, :] - top)
            p_ref[at, :] = e
            acc_ref[...] += dot(win_ref[at, HD:], e.astype(jnp.bfloat16), TN)
            return total + jnp.sum(e, axis=0, keepdims=True)

        total = lax.fori_loop(0, n_chunks, out_step, jnp.zeros((1, rows), jnp.float32))
        inverse = 1.0 / total
        summed = acc_ref[...] * inverse
        delta = jnp.sum(summed * dt_both[h].astype(jnp.float32), axis=0, keepdims=True)
        row_ref[...] = jnp.transpose(summed)
        for t in range(GROUP):
            mine_ref[h * GROUP + t] = row_ref[
                pl.ds(t * pair_len + own_at, block_len), :
            ].astype(jnp.bfloat16)
            back_ref[h * GROUP + t] = row_ref[
                pl.ds(t * pair_len + partner_at, block_len), :
            ].astype(jnp.bfloat16)

        acc_ref[...] = jnp.zeros_like(acc_ref)

        def grad_step(i, value_total):
            at = window(i)
            p = p_ref[at, :] * inverse
            dp = dot(win_ref[at, HD:], d_rows[...], NT)
            ds = (p * (dp - delta)).astype(jnp.bfloat16)
            value_part = dot(p.astype(jnp.bfloat16), d_rows[...], NN)
            grad_ref[at, HD:] = value_part
            grad_ref[at, :HD] = dot(ds, q_rows[...], NN) * scale
            acc_ref[...] += dot(win_ref[at, :HD], ds, TN)
            return value_total + jnp.sum(value_part, axis=0, keepdims=True)

        value_total = lax.fori_loop(0, n_chunks, grad_step, jnp.zeros((1, HD), jnp.float32))
        sum_ref[GROUP : GROUP + 1, :] += value_total
        row_ref[...] = jnp.transpose(acc_ref[...] * scale)
        for t in range(GROUP):
            mine_ref[(2 + h) * GROUP + t] = row_ref[
                pl.ds(t * pair_len + own_at, block_len), :
            ].astype(jnp.bfloat16)
            back_ref[(2 + h) * GROUP + t] = row_ref[
                pl.ds(t * pair_len + partner_at, block_len), :
            ].astype(jnp.bfloat16)
            sum_ref[t : t + 1, :] += jnp.sum(
                row_ref[t * pair_len : (t + 1) * pair_len, :], axis=0, keepdims=True
            )

        def store(i, carry):
            slot = place(low + i)
            part = grad_ref[pl.ds(pl.multiple_of(i * block_len, block_len), block_len), :]
            stage_ref[slot, :block_len, :] = (
                stage_ref[slot, :block_len, :].astype(jnp.float32) + part
            ).astype(jnp.bfloat16)
            return carry

        lax.fori_loop(0, n_blocks, store, 0)
        return carry

    lax.fori_loop(0, 2, query_unit, 0)

    sums = sum_ref[...]
    high = sums.astype(jnp.bfloat16).astype(jnp.float32)
    middle = (sums - high).astype(jnp.bfloat16).astype(jnp.float32)
    lowest = sums - high - middle
    pieces = jnp.concatenate(
        [
            jnp.concatenate([high, middle], axis=1),
            jnp.concatenate([lowest, jnp.zeros_like(lowest)], axis=1),
        ],
        axis=0,
    ).astype(jnp.bfloat16)
    for d in range(group_size):
        stage_ref[d, block_len:, :] = pieces
    for ref, late in ((mine_ref, own_late), (back_ref, other_late)):
        ref[4 * GROUP] = stage_ref[late, :block_len, :HD]
        ref[4 * GROUP + 1] = stage_ref[late, :block_len, HD:]
    stores = [
        pltpu.make_async_copy(source, into, out_sems.at[i])
        for i, (source, into) in enumerate(
            (
                (back_ref, back_hbm),
                (stage_ref.at[near, :block_len], near_grad_hbm),
                (stage_ref.at[far, :block_len], far_grad_hbm),
                (stage_ref.at[:group_size], parts_hbm),
                (mine_ref, mine_hbm),
            )
        )
    ]
    for store in stores:
        store.start()
    for store in stores:
        store.wait()


def join_kernel(
    me_ref, mine_ref, theirs_ref, near_hbm, far_hbm, att_ref, qg_ref, own_ref, theirs_late_ref
):
    head = me_ref[0] % 2
    for i, ref in enumerate((att_ref, qg_ref)):
        for h in range(2):
            for t in range(GROUP):
                tile = (2 * i + h) * GROUP + t
                ref[h, :, lanes(head * HALF_Q + t * HD, HD)] = mine_ref[tile]
                ref[h, :, lanes((1 - head) * HALF_Q + t * HD, HD)] = theirs_ref[tile]
    for ref, late_ref in ((mine_ref, own_ref), (theirs_ref, theirs_late_ref)):
        late_ref[:, :HD] = ref[4 * GROUP]
        late_ref[:, HD:] = ref[4 * GROUP + 1]


def total_kernel(
    group_size,
    reach,
    me_ref,
    got_ref,
    near_ref,
    far_ref,
    own_ref,
    theirs_ref,
    relay_ref,
    total_ref,
    sum_ref,
    acc_ref,
):
    block_len = total_ref.shape[2]
    me = me_ref[0]
    head = me % 2
    half = SUM_ROWS // 2
    acc_ref[2] = jnp.zeros_like(acc_ref[2])
    acc_ref[0, head] = near_ref[...].astype(jnp.float32)
    acc_ref[0, 1 - head] = far_ref[...].astype(jnp.float32)
    acc_ref[1, head] = own_ref[...].astype(jnp.float32)
    acc_ref[1, 1 - head] = theirs_ref[...].astype(jnp.float32)
    for d in range(group_size):
        kind = route(me, jnp.int32(d), group_size, reach)
        acc_ref[kind, d % KVH] += got_ref[d, :block_len, :].astype(jnp.float32)
    total_ref[...] = acc_ref[:2]
    relay_ref[...] = acc_ref[2].astype(jnp.bfloat16)
    for g in range(KVH):
        pieces = got_ref[g, block_len:, :].astype(jnp.float32)
        for d in range(g + KVH, group_size, KVH):
            pieces += got_ref[d, block_len:, :].astype(jnp.float32)
        sum_ref[g * half : (g + 1) * half, :] = (
            pieces[:half, :HD] + pieces[:half, HD:] + pieces[half:, :HD]
        )


def finish_kernel(total_ref, relay_ref, kg_ref, vg_ref):
    for g in range(KVH):
        cols = slice(g * HD, (g + 1) * HD)
        early = total_ref[0, g] + relay_ref[g].astype(jnp.float32)
        for h, total in enumerate((early, total_ref[1, g])):
            total = total.astype(jnp.bfloat16)
            kg_ref[h, :, cols] = total[:, :HD]
            vg_ref[h, :, cols] = total[:, HD:]


def bias_kernel(dp_ref, own_ref, *refs):
    *others, q_sum_ref, v_sum_ref, all_ref = refs
    me = dp_ref[0]
    for step, ref in enumerate((own_ref, *others)):
        all_ref[me ^ step] = ref[...]
    total = all_ref[0]
    for i in range(1, all_ref.shape[0]):
        total = total + all_ref[i]
    half = SUM_ROWS // 2
    for g in range(KVH):
        for t in range(GROUP):
            at = (g * GROUP + t) * HD
            q_sum_ref[:, at : at + HD] = total[g * half + t : g * half + t + 1]
        v_sum_ref[:, g * HD : (g + 1) * HD] = total[g * half + GROUP : (g + 1) * half]


def on_device(q_proj, k_proj, v_proj, q_bias, v_bias, cotangent, lengths):
    group_size = lax.axis_size("ctx")
    me = lax.axis_index("ctx").astype(jnp.int32)[None]
    q, ct, k, v = q_proj[0], cotangent[0], k_proj[0], v_proj[0]
    block_len = q.shape[1]
    reach = MOST // block_len
    rows = GROUP * 2 * block_len
    window = -(-(reach + 2) // BLOCKS_PER_CHUNK) * BLOCKS_PER_CHUNK * block_len
    bf16, f32 = jnp.bfloat16, jnp.float32
    more_tiles = jax.ShapeDtypeStruct((4 * GROUP + 2, block_len, HD), bf16)
    block = jax.ShapeDtypeStruct((block_len, SLOT_W), bf16)
    by_head = jax.ShapeDtypeStruct((KVH, block_len, SLOT_W), bf16)
    small = pltpu.CompilerParams(vmem_limit_bytes=SMALL_BYTES)
    large = pltpu.CompilerParams(vmem_limit_bytes=VMEM_BYTES)

    partners = [(i, i ^ 1) for i in range(group_size)]
    relays = [(i, group_size - 1 - i) for i in range(group_size - group_size // 4, group_size)]
    to_near, to_far = [], []
    for p in range(group_size // 2, group_size - group_size // 4, 2):
        lowest_late = 2 * group_size - 2 - p - reach
        for g in range(2):
            to_near.append((lowest_late + g, p + g))
            to_far.append((lowest_late + 1 - g, p + g))

    half_cols = (2, block_len, HALF_Q)
    row_pairs = jax.ShapeDtypeStruct((2, rows, HD), bf16)
    early, late, near, far = pl.pallas_call(
        blocks_kernel,
        out_shape=(by_head, by_head, block, block),
        in_specs=[SMEM] + [ANY] * 3,
        out_specs=(VMEM,) * 4,
        scratch_shapes=[
            pltpu.VMEM(k.shape, bf16),
            pltpu.VMEM(k.shape, bf16),
            pltpu.VMEM((1, KW), f32),
            pltpu.SemaphoreType.DMA((3,)),
        ],
        compiler_params=large,
        name="blocks",
    )(me, k, v, v_bias[None])
    relayed = lax.ppermute(early, "ctx", relays)
    near = lax.ppermute(near, "ctx", to_near)
    far = lax.ppermute(far, "ctx", to_far)
    swap = pl.pallas_call(
        swap_kernel,
        out_shape=more_tiles,
        in_specs=[SMEM, ANY, ANY, ANY],
        out_specs=VMEM,
        scratch_shapes=[
            pltpu.VMEM(half_cols, bf16),
            pltpu.VMEM(half_cols, bf16),
            pltpu.VMEM(block.shape, bf16),
            pltpu.SemaphoreType.DMA((3,)),
        ],
        compiler_params=large,
        cost_estimate=pl.CostEstimate(
            flops=SWAP_FLOPS, bytes_accessed=2_000_000, transcendentals=0
        ),
        name="swap",
    )(me, q, ct, late)
    other = lax.ppermute(swap, "ctx", partners)
    sent = pl.pallas_call(
        functools.partial(send_kernel, group_size, reach),
        out_shape=jax.ShapeDtypeStruct((group_size, block_len, SLOT_W), bf16),
        in_specs=[SMEM] + [VMEM] * 3 + [ANY] * 2,
        out_specs=ANY,
        scratch_shapes=[
            pltpu.VMEM((3, KVH, block_len, SLOT_W), bf16),
            pltpu.SemaphoreType.DMA((group_size,)),
        ],
        compiler_params=small,
        name="send",
    )(me, early, late, relayed, near, far)
    gathered = lax.all_to_all(sent, "ctx", 0, 0)
    q_rows, d_rows, d_cols = pl.pallas_call(
        prepare_kernel,
        out_shape=(row_pairs, row_pairs, jax.ShapeDtypeStruct((2, HD, rows), bf16)),
        in_specs=[SMEM] + [VMEM] * 4,
        out_specs=(VMEM,) * 3,
        cost_estimate=pl.CostEstimate(
            flops=PREP_FLOPS, bytes_accessed=4_000_000, transcendentals=0
        ),
        compiler_params=small,
        name="prepare",
    )(me, q, ct, other, q_bias[None])

    slot_len = block_len + SUM_ROWS
    mine, back, parts, near_grad, far_grad = pl.pallas_call(
        functools.partial(attention_kernel, group_size, reach),
        out_shape=(
            more_tiles,
            more_tiles,
            jax.ShapeDtypeStruct((group_size, slot_len, SLOT_W), bf16),
            block,
            block,
        ),
        in_specs=[SMEM, SMEM] + [ANY] * 8,
        out_specs=(ANY,) * 5,
        scratch_shapes=[
            pltpu.VMEM((2, block_len, HD), bf16),
            pltpu.VMEM(more_tiles.shape, bf16),
            pltpu.VMEM(more_tiles.shape, bf16),
            pltpu.VMEM((group_size + 4, block_len, SLOT_W), bf16),
            pltpu.VMEM((group_size + 4, slot_len, SLOT_W), bf16),
            pltpu.VMEM((window, SLOT_W), bf16),
            pltpu.VMEM(row_pairs.shape, bf16),
            pltpu.VMEM(row_pairs.shape, bf16),
            pltpu.VMEM((2, HD, rows), bf16),
            pltpu.VMEM((window, rows), f32),
            pltpu.VMEM((window, SLOT_W), f32),
            pltpu.VMEM((HD, rows), f32),
            pltpu.VMEM((rows, HD), f32),
            pltpu.VMEM((SUM_ROWS // 2, HD), f32),
            pltpu.SemaphoreType.DMA((8,)),
            pltpu.SemaphoreType.DMA((5,)),
        ],
        compiler_params=large,
        cost_estimate=pl.CostEstimate(
            flops=3_000_000_000, bytes_accessed=10_000_000, transcendentals=2_000_000
        ),
        name="attention",
    )(me, lengths, q_rows, d_rows, d_cols, other, gathered, late, near, far)

    def back_along(pairs):
        return [(target, source) for source, target in pairs]

    theirs = lax.ppermute(back, "ctx", partners)
    near_grad = lax.ppermute(near_grad, "ctx", back_along(to_near))
    far_grad = lax.ppermute(far_grad, "ctx", back_along(to_far))
    got = lax.all_to_all(parts, "ctx", 0, 0)
    wide = jax.ShapeDtypeStruct(q.shape, bf16)
    narrow = jax.ShapeDtypeStruct(k.shape, bf16)
    attended, q_grad, own, theirs_late = pl.pallas_call(
        join_kernel,
        out_shape=(wide, wide, block, block),
        in_specs=[SMEM, VMEM, VMEM, ANY, ANY],
        out_specs=(VMEM,) * 4,
        cost_estimate=pl.CostEstimate(
            flops=JOIN_FLOPS, bytes_accessed=4_000_000, transcendentals=0
        ),
        compiler_params=small,
        name="join",
    )(me, mine, theirs, near_grad, far_grad)
    relay_total, total, sums = pl.pallas_call(
        functools.partial(total_kernel, group_size, reach),
        out_shape=(
            by_head,
            jax.ShapeDtypeStruct((2, KVH, block_len, SLOT_W), f32),
            jax.ShapeDtypeStruct((SUM_ROWS, HD), f32),
        ),
        in_specs=[SMEM] + [VMEM] * 5,
        out_specs=(VMEM, VMEM, VMEM),
        scratch_shapes=[pltpu.VMEM((3, KVH, block_len, SLOT_W), f32)],
        compiler_params=small,
        name="total",
    )(me, got, near_grad, far_grad, own, theirs_late)
    relay_grad = lax.ppermute(relay_total, "ctx", back_along(relays))
    dp_size = lax.axis_size("dp")
    dp_me = lax.axis_index("dp").astype(jnp.int32)[None]
    other_sums = [
        lax.ppermute(sums, "dp", [(i, i ^ step) for i in range(dp_size)])
        for step in range(1, dp_size)
    ]
    k_grad, v_grad = pl.pallas_call(
        finish_kernel,
        out_shape=(narrow, narrow),
        in_specs=[VMEM, VMEM],
        out_specs=(VMEM, VMEM),
        cost_estimate=pl.CostEstimate(
            flops=FINISH_FLOPS, bytes_accessed=1_000_000, transcendentals=0
        ),
        compiler_params=small,
        name="finish",
    )(total, relay_grad)
    q_sum, v_sum = pl.pallas_call(
        bias_kernel,
        out_shape=(jax.ShapeDtypeStruct((1, HQ), f32), jax.ShapeDtypeStruct((1, KW), f32)),
        in_specs=[SMEM] + [VMEM] * dp_size,
        out_specs=(VMEM, VMEM),
        scratch_shapes=[pltpu.VMEM((dp_size, SUM_ROWS, HD), f32)],
        cost_estimate=pl.CostEstimate(
            flops=BIAS_FLOPS, bytes_accessed=100_000, transcendentals=0
        ),
        compiler_params=small,
        name="bias",
    )(dp_me, sums, *other_sums)
    return (
        attended[None],
        q_grad[None],
        k_grad[None],
        v_grad[None],
        q_sum.reshape(HQ),
        v_sum.reshape(KW),
    )


def solution(mesh):
    placed = (
        P("dp", None, "ctx", None),
        P("dp", None, "ctx", None),
        P("dp", None, "ctx", None),
        P(),
        P(),
        P("dp", None, "ctx", None),
        P("dp", None),
    )
    return jax.shard_map(
        on_device,
        mesh=mesh,
        in_specs=placed,
        out_specs=(
            P("dp", None, "ctx", None),
            P("dp", None, "ctx", None),
            P("dp", None, "ctx", None),
            P("dp", None, "ctx", None),
            P(),
            P(),
        ),
        check_vma=False,
    )
```

```python
import functools
import math

import jax
import jax.numpy as jnp
from jax import lax
from jax.experimental import pallas as pl
from jax.experimental.pallas import tpu as pltpu
from jax.sharding import PartitionSpec as P

HD = 128
KVH = 2
GROUP = 7
HQ = 1792
KW = 256
MOST = 1024

HALF_Q = GROUP * HD
SLOT_W = 2 * HD
SUM_ROWS = 16
MASKED = -1e30
PREP_FLOPS = 5_600_000_000
SWAP_FLOPS = 1_000_000
JOIN_FLOPS = 40_000_000_000
FINISH_FLOPS = 1_000_000
BIAS_FLOPS = 10_000_000_000
VMEM_BYTES = 59 * 1024 * 1024
SMALL_BYTES = 16 * 1024 * 1024
BLOCKS_PER_CHUNK = 9

NT = (((1,), (1,)), ((), ()))
NN = (((1,), (0,)), ((), ()))
TN = (((0,), (0,)), ((), ()))

SMEM = pl.BlockSpec(memory_space=pltpu.SMEM)
VMEM = pl.BlockSpec(memory_space=pltpu.VMEM)
ANY = pl.BlockSpec(memory_space=pl.ANY)


def dot(a, b, dims):
    return lax.dot_general(a, b, dims, preferred_element_type=jnp.float32)


def lanes(start, size):
    return pl.ds(pl.multiple_of(start, HD), size)


def route(c, d, group_size, reach):
    pair = d - d % 2
    late = (c > pair + 1) & (c <= pair + reach + 1)
    relay = (c < pair - reach) & (c <= group_size - 3 - pair)
    return jnp.where(late, 1, jnp.where(relay, 2, 0))


def blocks_kernel(me_ref, k_hbm, v_hbm, vb_hbm, early_ref, late_ref, near_ref, far_ref, k_ref, v_ref, vb_ref, sems):
    head = me_ref[0] % 2
    pairs = ((k_hbm, k_ref), (v_hbm, v_ref), (vb_hbm, vb_ref))
    loads = [
        pltpu.make_async_copy(source, into, sems.at[i]) for i, (source, into) in enumerate(pairs)
    ]
    for load in loads:
        load.start()
    for load in loads:
        load.wait()
    for h, ref in enumerate((early_ref, late_ref)):
        for g in range(KVH):
            cols = slice(g * HD, (g + 1) * HD)
            ref[g, :, :HD] = k_ref[h, :, cols]
            ref[g, :, HD:] = (v_ref[h, :, cols].astype(jnp.float32) + vb_ref[:, cols]).astype(
                jnp.bfloat16
            )
    near_ref[...] = early_ref[head]
    far_ref[...] = early_ref[1 - head]


def swap_kernel(me_ref, q_hbm, ct_hbm, late_hbm, swap_ref, q_ref, ct_ref, late_ref, sems):
    other = 1 - me_ref[0] % 2
    cols = lanes(other * HALF_Q, HALF_Q)
    pairs = ((q_hbm.at[:, :, cols], q_ref), (ct_hbm.at[:, :, cols], ct_ref), (late_hbm.at[other], late_ref))
    loads = [
        pltpu.make_async_copy(source, into, sems.at[i]) for i, (source, into) in enumerate(pairs)
    ]
    for load in loads:
        load.start()
    for i, ref in enumerate((q_ref, ct_ref)):
        loads[i].wait()
        for h in range(2):
            for t in range(GROUP):
                swap_ref[(2 * i + h) * GROUP + t] = ref[h, :, t * HD : (t + 1) * HD]
    loads[2].wait()
    swap_ref[4 * GROUP] = late_ref[:, :HD]
    swap_ref[4 * GROUP + 1] = late_ref[:, HD:]


def prepare_kernel(
    me_ref, q_ref, ct_ref, other_ref, qb_ref, q_rows, d_rows, d_cols
):
    block_len = q_ref.shape[1]
    pair_len = 2 * block_len
    head = me_ref[0] % 2
    for h in range(2):
        own_at = pl.multiple_of((head if h == 0 else 1 - head) * block_len, block_len)
        partner_at = pl.multiple_of(block_len - own_at, block_len)
        for t in range(GROUP):
            own_lanes = lanes(head * HALF_Q + t * HD, HD)
            bias = qb_ref[:, own_lanes]
            own_rows = pl.ds(t * pair_len + own_at, block_len)
            partner_rows = pl.ds(t * pair_len + partner_at, block_len)
            q_rows[h, own_rows, :] = (q_ref[h, :, own_lanes].astype(jnp.float32) + bias).astype(
                jnp.bfloat16
            )
            q_rows[h, partner_rows, :] = (
                other_ref[h * GROUP + t].astype(jnp.float32) + bias
            ).astype(jnp.bfloat16)
            d_rows[h, own_rows, :] = ct_ref[h, :, own_lanes]
            d_rows[h, partner_rows, :] = other_ref[(2 + h) * GROUP + t]
        d_cols[h] = jnp.transpose(d_rows[h].astype(jnp.float32)).astype(jnp.bfloat16)


def send_kernel(
    group_size, reach, me_ref, early_ref, late_ref, relay_ref, near_hbm, far_hbm, send_ref, all_ref, sem
):
    me = me_ref[0]
    all_ref[0] = early_ref[...]
    all_ref[1] = late_ref[...]
    all_ref[2] = relay_ref[...]
    copies = []
    for d in range(group_size):
        kind = route(me, jnp.int32(d), group_size, reach)
        copy = pltpu.make_async_copy(all_ref.at[kind, d % KVH], send_ref.at[d], sem.at[d])
        copy.start()
        copies.append(copy)
    for copy in copies:
        copy.wait()


def attention_kernel(
    group_size,
    reach,
    me_ref,
    len_ref,
    q_hbm,
    d_hbm,
    dt_hbm,
    other_hbm,
    kv_hbm,
    late_hbm,
    near_hbm,
    far_hbm,
    mine_hbm,
    back_hbm,
    parts_hbm,
    near_grad_hbm,
    far_grad_hbm,
    other_ref,
    mine_ref,
    back_ref,
    all_ref,
    stage_ref,
    win_ref,
    q_both,
    d_both,
    dt_both,
    p_ref,
    grad_ref,
    acc_ref,
    row_ref,
    sum_ref,
    in_sems,
    out_sems,
    tile_sems,
):
    block_len = mine_ref.shape[1]
    pair_len = 2 * block_len
    rows = GROUP * pair_len
    chunk = BLOCKS_PER_CHUNK * block_len
    scale = 1.0 / math.sqrt(HD)
    log2e = 1.0 / math.log(2.0)
    last_block = 2 * group_size - 1
    me = me_ref[0]
    head = me % 2
    pair = me - head
    n_docs = len_ref.shape[1]
    own_late, other_late, near, far = range(group_size, group_size + 4)

    loads = [
        pltpu.make_async_copy(source, into, in_sems.at[i])
        for i, (source, into) in enumerate(
            (
                (other_hbm.at[4 * GROUP :], other_ref),
                (q_hbm, q_both),
                (d_hbm, d_both),
                (dt_hbm, dt_both),
                (kv_hbm, all_ref.at[:group_size]),
                (late_hbm.at[head], all_ref.at[own_late]),
                (near_hbm, all_ref.at[near]),
                (far_hbm, all_ref.at[far]),
            )
        )
    ]
    for load in loads:
        load.start()

    def place(block):
        lowest_late = last_block - 1 - pair - reach
        doubled = jnp.where(
            group_size - 1 - block < pair - reach,
            group_size - 1 - block,
            jnp.where(block == lowest_late + head, near, far),
        )
        early = jnp.where(block <= pair + 1, block, doubled)
        c = last_block - block
        late = jnp.where(c == me, own_late, jnp.where(c == pair + 1 - head, other_late, c))
        return jnp.where(block < group_size, early, late)

    def tile_copies(first, count, sem):
        at = pl.ds(first, count)
        return [
            pltpu.make_async_copy(ref.at[at], hbm.at[at], tile_sems.at[i, sem])
            for i, (ref, hbm) in enumerate(((back_ref, back_hbm), (mine_ref, mine_hbm)))
        ]

    stage_ref[...] = jnp.zeros_like(stage_ref)
    sum_ref[...] = jnp.zeros_like(sum_ref)
    for load in loads:
        load.wait()
    all_ref[other_late, :, :HD] = other_ref[0]
    all_ref[other_late, :, HD:] = other_ref[1]

    def query_unit(h, carry):
        first_block = jnp.where(h == 0, pair, last_block - 1 - pair)
        first_pos = first_block * block_len
        own_at = pl.multiple_of(jnp.where(h == 0, head, 1 - head) * block_len, block_len)
        partner_at = pl.multiple_of(block_len - own_at, block_len)
        lane = lax.broadcasted_iota(jnp.int32, (1, rows), 1)
        query_pos = first_pos + lane % pair_len
        query_start = jnp.zeros_like(query_pos)
        end = jnp.int32(0)
        first_start = jnp.int32(0)
        for k in range(n_docs):
            end = end + len_ref[0, k]
            query_start = jnp.where(query_pos >= end, end, query_start)
            first_start = jnp.where(first_pos >= end, end, first_start)
        low = first_start // block_len
        n_blocks = first_block + 2 - low
        n_chunks = (n_blocks + BLOCKS_PER_CHUNK - 1) // BLOCKS_PER_CHUNK

        def load(i, carry):
            win_ref[pl.ds(pl.multiple_of(i * block_len, block_len), block_len), :] = all_ref[
                place(jnp.minimum(low + i, first_block + 1))
            ]
            return carry

        lax.fori_loop(0, n_chunks * BLOCKS_PER_CHUNK, load, 0)

        q_rows, d_rows = q_both.at[h], d_both.at[h]

        def window(i):
            return pl.ds(pl.multiple_of(i * chunk, chunk), chunk)

        def score_step(i, top):
            at = window(i)
            s = dot(win_ref[at, :HD], q_rows[...], NT) * (scale * log2e)
            key_pos = (low * block_len + i * chunk) + lax.broadcasted_iota(
                jnp.int32, (chunk, 1), 0
            )
            visible = (key_pos >= query_start) & (key_pos <= query_pos)
            s = jnp.where(visible, s, MASKED)
            p_ref[at, :] = s
            return jnp.maximum(top, jnp.max(s, axis=0, keepdims=True))

        top = lax.fori_loop(0, n_chunks, score_step, jnp.full((1, rows), MASKED, jnp.float32))

        acc_ref[...] = jnp.zeros_like(acc_ref)

        def out_step(i, total):
            at = window(i)
            e = jnp.exp2(p_ref[at, :] - top)
            p_ref[at, :] = e
            acc_ref[...] += dot(win_ref[at, HD:], e.astype(jnp.bfloat16), TN)
            return total + jnp.sum(e, axis=0, keepdims=True)

        total = lax.fori_loop(0, n_chunks, out_step, jnp.zeros((1, rows), jnp.float32))
        inverse = 1.0 / total
        summed = acc_ref[...] * inverse
        delta = jnp.sum(summed * dt_both[h].astype(jnp.float32), axis=0, keepdims=True)
        row_ref[...] = jnp.transpose(summed)
        for t in range(GROUP):
            mine_ref[h * GROUP + t] = row_ref[
                pl.ds(t * pair_len + own_at, block_len), :
            ].astype(jnp.bfloat16)
            back_ref[h * GROUP + t] = row_ref[
                pl.ds(t * pair_len + partner_at, block_len), :
            ].astype(jnp.bfloat16)

        for copy in tile_copies(h * GROUP, GROUP, h):
            copy.start()
        acc_ref[...] = jnp.zeros_like(acc_ref)

        def grad_step(i, value_total):
            at = window(i)
            p = p_ref[at, :] * inverse
            dp = dot(win_ref[at, HD:], d_rows[...], NT)
            ds = (p * (dp - delta)).astype(jnp.bfloat16)
            value_part = dot(p.astype(jnp.bfloat16), d_rows[...], NN)
            grad_ref[at, HD:] = value_part
            grad_ref[at, :HD] = dot(ds, q_rows[...], NN) * scale
            acc_ref[...] += dot(win_ref[at, :HD], ds, TN)
            return value_total + jnp.sum(value_part, axis=0, keepdims=True)

        value_total = lax.fori_loop(0, n_chunks, grad_step, jnp.zeros((1, HD), jnp.float32))
        sum_ref[GROUP : GROUP + 1, :] += value_total
        row_ref[...] = jnp.transpose(acc_ref[...] * scale)
        for t in range(GROUP):
            mine_ref[(2 + h) * GROUP + t] = row_ref[
                pl.ds(t * pair_len + own_at, block_len), :
            ].astype(jnp.bfloat16)
            back_ref[(2 + h) * GROUP + t] = row_ref[
                pl.ds(t * pair_len + partner_at, block_len), :
            ].astype(jnp.bfloat16)
            sum_ref[t : t + 1, :] += jnp.sum(
                row_ref[t * pair_len : (t + 1) * pair_len, :], axis=0, keepdims=True
            )

        for copy in tile_copies((2 + h) * GROUP, GROUP, 2 + h):
            copy.start()

        def store(i, carry):
            slot = place(low + i)
            part = grad_ref[pl.ds(pl.multiple_of(i * block_len, block_len), block_len), :]
            stage_ref[slot, :block_len, :] = (
                stage_ref[slot, :block_len, :].astype(jnp.float32) + part
            ).astype(jnp.bfloat16)
            return carry

        lax.fori_loop(0, n_blocks, store, 0)
        return carry

    lax.fori_loop(0, 2, query_unit, 0)

    sums = sum_ref[...]
    high = sums.astype(jnp.bfloat16).astype(jnp.float32)
    middle = (sums - high).astype(jnp.bfloat16).astype(jnp.float32)
    lowest = sums - high - middle
    pieces = jnp.concatenate(
        [
            jnp.concatenate([high, middle], axis=1),
            jnp.concatenate([lowest, jnp.zeros_like(lowest)], axis=1),
        ],
        axis=0,
    ).astype(jnp.bfloat16)
    for d in range(group_size):
        stage_ref[d, block_len:, :] = pieces
    for ref, late in ((mine_ref, own_late), (back_ref, other_late)):
        ref[4 * GROUP] = stage_ref[late, :block_len, :HD]
        ref[4 * GROUP + 1] = stage_ref[late, :block_len, HD:]
    stores = [
        pltpu.make_async_copy(source, into, out_sems.at[i])
        for i, (source, into) in enumerate(
            (
                (stage_ref.at[near, :block_len], near_grad_hbm),
                (stage_ref.at[far, :block_len], far_grad_hbm),
                (stage_ref.at[:group_size], parts_hbm),
            )
        )
    ] + tile_copies(4 * GROUP, 2, 4)
    for store in stores:
        store.start()
    for i in range(4):
        stores += tile_copies(i * GROUP, GROUP, i)
    for store in stores:
        store.wait()


def join_kernel(
    me_ref, mine_ref, theirs_ref, near_hbm, far_hbm, att_ref, qg_ref, own_ref, theirs_late_ref
):
    head = me_ref[0] % 2
    for i, ref in enumerate((att_ref, qg_ref)):
        for h in range(2):
            for t in range(GROUP):
                tile = (2 * i + h) * GROUP + t
                ref[h, :, lanes(head * HALF_Q + t * HD, HD)] = mine_ref[tile]
                ref[h, :, lanes((1 - head) * HALF_Q + t * HD, HD)] = theirs_ref[tile]
    for ref, late_ref in ((mine_ref, own_ref), (theirs_ref, theirs_late_ref)):
        late_ref[:, :HD] = ref[4 * GROUP]
        late_ref[:, HD:] = ref[4 * GROUP + 1]


def total_kernel(
    group_size,
    reach,
    me_ref,
    got_ref,
    near_ref,
    far_ref,
    own_ref,
    theirs_ref,
    relay_ref,
    total_ref,
    sum_ref,
    acc_ref,
):
    block_len = total_ref.shape[2]
    me = me_ref[0]
    head = me % 2
    half = SUM_ROWS // 2
    acc_ref[2] = jnp.zeros_like(acc_ref[2])
    acc_ref[0, head] = near_ref[...].astype(jnp.float32)
    acc_ref[0, 1 - head] = far_ref[...].astype(jnp.float32)
    acc_ref[1, head] = own_ref[...].astype(jnp.float32)
    acc_ref[1, 1 - head] = theirs_ref[...].astype(jnp.float32)
    for d in range(group_size):
        kind = route(me, jnp.int32(d), group_size, reach)
        acc_ref[kind, d % KVH] += got_ref[d, :block_len, :].astype(jnp.float32)
    total_ref[...] = acc_ref[:2]
    relay_ref[...] = acc_ref[2].astype(jnp.bfloat16)
    for g in range(KVH):
        pieces = got_ref[g, block_len:, :].astype(jnp.float32)
        for d in range(g + KVH, group_size, KVH):
            pieces += got_ref[d, block_len:, :].astype(jnp.float32)
        sum_ref[g * half : (g + 1) * half, :] = (
            pieces[:half, :HD] + pieces[:half, HD:] + pieces[half:, :HD]
        )


def finish_kernel(total_ref, relay_ref, kg_ref, vg_ref):
    for g in range(KVH):
        cols = slice(g * HD, (g + 1) * HD)
        early = total_ref[0, g] + relay_ref[g].astype(jnp.float32)
        for h, total in enumerate((early, total_ref[1, g])):
            total = total.astype(jnp.bfloat16)
            kg_ref[h, :, cols] = total[:, :HD]
            vg_ref[h, :, cols] = total[:, HD:]


def bias_kernel(dp_ref, own_ref, *refs):
    *others, q_sum_ref, v_sum_ref, all_ref = refs
    me = dp_ref[0]
    for step, ref in enumerate((own_ref, *others)):
        all_ref[me ^ step] = ref[...]
    total = all_ref[0]
    for i in range(1, all_ref.shape[0]):
        total = total + all_ref[i]
    half = SUM_ROWS // 2
    for g in range(KVH):
        for t in range(GROUP):
            at = (g * GROUP + t) * HD
            q_sum_ref[:, at : at + HD] = total[g * half + t : g * half + t + 1]
        v_sum_ref[:, g * HD : (g + 1) * HD] = total[g * half + GROUP : (g + 1) * half]


def on_device(q_proj, k_proj, v_proj, q_bias, v_bias, cotangent, lengths):
    group_size = lax.axis_size("ctx")
    me = lax.axis_index("ctx").astype(jnp.int32)[None]
    q, ct, k, v = q_proj[0], cotangent[0], k_proj[0], v_proj[0]
    block_len = q.shape[1]
    reach = MOST // block_len
    rows = GROUP * 2 * block_len
    window = -(-(reach + 2) // BLOCKS_PER_CHUNK) * BLOCKS_PER_CHUNK * block_len
    bf16, f32 = jnp.bfloat16, jnp.float32
    more_tiles = jax.ShapeDtypeStruct((4 * GROUP + 2, block_len, HD), bf16)
    block = jax.ShapeDtypeStruct((block_len, SLOT_W), bf16)
    by_head = jax.ShapeDtypeStruct((KVH, block_len, SLOT_W), bf16)
    small = pltpu.CompilerParams(vmem_limit_bytes=SMALL_BYTES)
    large = pltpu.CompilerParams(vmem_limit_bytes=VMEM_BYTES)

    partners = [(i, i ^ 1) for i in range(group_size)]
    relays = [(i, group_size - 1 - i) for i in range(group_size - group_size // 4, group_size)]
    to_near, to_far = [], []
    for p in range(group_size // 2, group_size - group_size // 4, 2):
        lowest_late = 2 * group_size - 2 - p - reach
        for g in range(2):
            to_near.append((lowest_late + g, p + g))
            to_far.append((lowest_late + 1 - g, p + g))

    half_cols = (2, block_len, HALF_Q)
    row_pairs = jax.ShapeDtypeStruct((2, rows, HD), bf16)
    early, late, near, far = pl.pallas_call(
        blocks_kernel,
        out_shape=(by_head, by_head, block, block),
        in_specs=[SMEM] + [ANY] * 3,
        out_specs=(VMEM,) * 4,
        scratch_shapes=[
            pltpu.VMEM(k.shape, bf16),
            pltpu.VMEM(k.shape, bf16),
            pltpu.VMEM((1, KW), f32),
            pltpu.SemaphoreType.DMA((3,)),
        ],
        compiler_params=large,
        name="blocks",
    )(me, k, v, v_bias[None])
    relayed = lax.ppermute(early, "ctx", relays)
    near = lax.ppermute(near, "ctx", to_near)
    far = lax.ppermute(far, "ctx", to_far)
    swap = pl.pallas_call(
        swap_kernel,
        out_shape=more_tiles,
        in_specs=[SMEM, ANY, ANY, ANY],
        out_specs=VMEM,
        scratch_shapes=[
            pltpu.VMEM(half_cols, bf16),
            pltpu.VMEM(half_cols, bf16),
            pltpu.VMEM(block.shape, bf16),
            pltpu.SemaphoreType.DMA((3,)),
        ],
        compiler_params=large,
        cost_estimate=pl.CostEstimate(
            flops=SWAP_FLOPS, bytes_accessed=2_000_000, transcendentals=0
        ),
        name="swap",
    )(me, q, ct, late)
    other = lax.ppermute(swap, "ctx", partners)
    sent = pl.pallas_call(
        functools.partial(send_kernel, group_size, reach),
        out_shape=jax.ShapeDtypeStruct((group_size, block_len, SLOT_W), bf16),
        in_specs=[SMEM] + [VMEM] * 3 + [ANY] * 2,
        out_specs=ANY,
        scratch_shapes=[
            pltpu.VMEM((3, KVH, block_len, SLOT_W), bf16),
            pltpu.SemaphoreType.DMA((group_size,)),
        ],
        compiler_params=small,
        name="send",
    )(me, early, late, relayed, near, far)
    gathered = lax.all_to_all(sent, "ctx", 0, 0)
    q_rows, d_rows, d_cols = pl.pallas_call(
        prepare_kernel,
        out_shape=(row_pairs, row_pairs, jax.ShapeDtypeStruct((2, HD, rows), bf16)),
        in_specs=[SMEM] + [VMEM] * 4,
        out_specs=(VMEM,) * 3,
        cost_estimate=pl.CostEstimate(
            flops=PREP_FLOPS, bytes_accessed=4_000_000, transcendentals=0
        ),
        compiler_params=small,
        name="prepare",
    )(me, q, ct, other, q_bias[None])

    slot_len = block_len + SUM_ROWS
    mine, back, parts, near_grad, far_grad = pl.pallas_call(
        functools.partial(attention_kernel, group_size, reach),
        out_shape=(
            more_tiles,
            more_tiles,
            jax.ShapeDtypeStruct((group_size, slot_len, SLOT_W), bf16),
            block,
            block,
        ),
        in_specs=[SMEM, SMEM] + [ANY] * 8,
        out_specs=(ANY,) * 5,
        scratch_shapes=[
            pltpu.VMEM((2, block_len, HD), bf16),
            pltpu.VMEM(more_tiles.shape, bf16),
            pltpu.VMEM(more_tiles.shape, bf16),
            pltpu.VMEM((group_size + 4, block_len, SLOT_W), bf16),
            pltpu.VMEM((group_size + 4, slot_len, SLOT_W), bf16),
            pltpu.VMEM((window, SLOT_W), bf16),
            pltpu.VMEM(row_pairs.shape, bf16),
            pltpu.VMEM(row_pairs.shape, bf16),
            pltpu.VMEM((2, HD, rows), bf16),
            pltpu.VMEM((window, rows), f32),
            pltpu.VMEM((window, SLOT_W), f32),
            pltpu.VMEM((HD, rows), f32),
            pltpu.VMEM((rows, HD), f32),
            pltpu.VMEM((SUM_ROWS // 2, HD), f32),
            pltpu.SemaphoreType.DMA((8,)),
            pltpu.SemaphoreType.DMA((3,)),
            pltpu.SemaphoreType.DMA((2, 5)),
        ],
        compiler_params=large,
        cost_estimate=pl.CostEstimate(
            flops=3_000_000_000, bytes_accessed=10_000_000, transcendentals=2_000_000
        ),
        name="attention",
    )(me, lengths, q_rows, d_rows, d_cols, other, gathered, late, near, far)

    def back_along(pairs):
        return [(target, source) for source, target in pairs]

    theirs = lax.ppermute(back, "ctx", partners)
    near_grad = lax.ppermute(near_grad, "ctx", back_along(to_near))
    far_grad = lax.ppermute(far_grad, "ctx", back_along(to_far))
    got = lax.all_to_all(parts, "ctx", 0, 0)
    wide = jax.ShapeDtypeStruct(q.shape, bf16)
    narrow = jax.ShapeDtypeStruct(k.shape, bf16)
    attended, q_grad, own, theirs_late = pl.pallas_call(
        join_kernel,
        out_shape=(wide, wide, block, block),
        in_specs=[SMEM, VMEM, VMEM, ANY, ANY],
        out_specs=(VMEM,) * 4,
        cost_estimate=pl.CostEstimate(
            flops=JOIN_FLOPS, bytes_accessed=4_000_000, transcendentals=0
        ),
        compiler_params=small,
        name="join",
    )(me, mine, theirs, near_grad, far_grad)
    relay_total, total, sums = pl.pallas_call(
        functools.partial(total_kernel, group_size, reach),
        out_shape=(
            by_head,
            jax.ShapeDtypeStruct((2, KVH, block_len, SLOT_W), f32),
            jax.ShapeDtypeStruct((SUM_ROWS, HD), f32),
        ),
        in_specs=[SMEM] + [VMEM] * 5,
        out_specs=(VMEM, VMEM, VMEM),
        scratch_shapes=[pltpu.VMEM((3, KVH, block_len, SLOT_W), f32)],
        compiler_params=small,
        name="total",
    )(me, got, near_grad, far_grad, own, theirs_late)
    relay_grad = lax.ppermute(relay_total, "ctx", back_along(relays))
    dp_size = lax.axis_size("dp")
    dp_me = lax.axis_index("dp").astype(jnp.int32)[None]
    other_sums = [
        lax.ppermute(sums, "dp", [(i, i ^ step) for i in range(dp_size)])
        for step in range(1, dp_size)
    ]
    k_grad, v_grad = pl.pallas_call(
        finish_kernel,
        out_shape=(narrow, narrow),
        in_specs=[VMEM, VMEM],
        out_specs=(VMEM, VMEM),
        cost_estimate=pl.CostEstimate(
            flops=FINISH_FLOPS, bytes_accessed=1_000_000, transcendentals=0
        ),
        compiler_params=small,
        name="finish",
    )(total, relay_grad)
    q_sum, v_sum = pl.pallas_call(
        bias_kernel,
        out_shape=(jax.ShapeDtypeStruct((1, HQ), f32), jax.ShapeDtypeStruct((1, KW), f32)),
        in_specs=[SMEM] + [VMEM] * dp_size,
        out_specs=(VMEM, VMEM),
        scratch_shapes=[pltpu.VMEM((dp_size, SUM_ROWS, HD), f32)],
        cost_estimate=pl.CostEstimate(
            flops=BIAS_FLOPS, bytes_accessed=100_000, transcendentals=0
        ),
        compiler_params=small,
        name="bias",
    )(dp_me, sums, *other_sums)
    return (
        attended[None],
        q_grad[None],
        k_grad[None],
        v_grad[None],
        q_sum.reshape(HQ),
        v_sum.reshape(KW),
    )


def solution(mesh):
    placed = (
        P("dp", None, "ctx", None),
        P("dp", None, "ctx", None),
        P("dp", None, "ctx", None),
        P(),
        P(),
        P("dp", None, "ctx", None),
        P("dp", None),
    )
    return jax.shard_map(
        on_device,
        mesh=mesh,
        in_specs=placed,
        out_specs=(
            P("dp", None, "ctx", None),
            P("dp", None, "ctx", None),
            P("dp", None, "ctx", None),
            P("dp", None, "ctx", None),
            P(),
            P(),
        ),
        check_vma=False,
    )
```

```python
import functools
import math

import jax
import jax.numpy as jnp
from jax import lax
from jax.experimental import pallas as pl
from jax.experimental.pallas import tpu as pltpu
from jax.sharding import PartitionSpec as P

HD = 128
KVH = 2
GROUP = 7
HQ = 1792
KW = 256
MOST = 1024

HALF_Q = GROUP * HD
SLOT_W = 2 * HD
SUM_ROWS = 16
MASKED = -1e30
PREP_FLOPS = 5_600_000_000
SWAP_FLOPS = 1_000_000
JOIN_FLOPS = 40_000_000_000
FINISH_FLOPS = 1_000_000
BIAS_FLOPS = 10_000_000_000
VMEM_BYTES = 59 * 1024 * 1024
SMALL_BYTES = 16 * 1024 * 1024
BLOCKS_PER_CHUNK = 9

NT = (((1,), (1,)), ((), ()))
NN = (((1,), (0,)), ((), ()))
TN = (((0,), (0,)), ((), ()))

SMEM = pl.BlockSpec(memory_space=pltpu.SMEM)
VMEM = pl.BlockSpec(memory_space=pltpu.VMEM)
ANY = pl.BlockSpec(memory_space=pl.ANY)


def dot(a, b, dims):
    return lax.dot_general(a, b, dims, preferred_element_type=jnp.float32)


def lanes(start, size):
    return pl.ds(pl.multiple_of(start, HD), size)


def route(c, d, group_size, reach):
    pair = d - d % 2
    late = (c > pair + 1) & (c <= pair + reach + 1)
    relay = (c < pair - reach) & (c <= group_size - 3 - pair)
    return jnp.where(late, 1, jnp.where(relay, 2, 0))


def blocks_kernel(me_ref, k_hbm, v_hbm, vb_hbm, early_ref, late_ref, near_ref, far_ref, k_ref, v_ref, vb_ref, sems):
    head = me_ref[0] % 2
    pairs = ((k_hbm, k_ref), (v_hbm, v_ref), (vb_hbm, vb_ref))
    loads = [
        pltpu.make_async_copy(source, into, sems.at[i]) for i, (source, into) in enumerate(pairs)
    ]
    for load in loads:
        load.start()
    for load in loads:
        load.wait()
    for h, ref in enumerate((early_ref, late_ref)):
        for g in range(KVH):
            cols = slice(g * HD, (g + 1) * HD)
            ref[g, :, :HD] = k_ref[h, :, cols]
            ref[g, :, HD:] = (v_ref[h, :, cols].astype(jnp.float32) + vb_ref[:, cols]).astype(
                jnp.bfloat16
            )
    near_ref[...] = early_ref[head]
    far_ref[...] = early_ref[1 - head]


def swap_kernel(me_ref, q_hbm, ct_hbm, late_hbm, swap_ref, q_ref, ct_ref, late_ref, sems):
    other = 1 - me_ref[0] % 2
    cols = lanes(other * HALF_Q, HALF_Q)
    pairs = ((q_hbm.at[:, :, cols], q_ref), (ct_hbm.at[:, :, cols], ct_ref), (late_hbm.at[other], late_ref))
    loads = [
        pltpu.make_async_copy(source, into, sems.at[i]) for i, (source, into) in enumerate(pairs)
    ]
    for load in loads:
        load.start()
    for i, ref in enumerate((q_ref, ct_ref)):
        loads[i].wait()
        for h in range(2):
            for t in range(GROUP):
                swap_ref[(2 * i + h) * GROUP + t] = ref[h, :, t * HD : (t + 1) * HD]
    loads[2].wait()
    swap_ref[4 * GROUP] = late_ref[:, :HD]
    swap_ref[4 * GROUP + 1] = late_ref[:, HD:]


def prepare_kernel(
    me_ref, q_ref, ct_ref, other_ref, qb_ref, q_rows, d_rows, d_cols
):
    block_len = q_ref.shape[1]
    pair_len = 2 * block_len
    head = me_ref[0] % 2
    for h in range(2):
        own_at = pl.multiple_of((head if h == 0 else 1 - head) * block_len, block_len)
        partner_at = pl.multiple_of(block_len - own_at, block_len)
        for t in range(GROUP):
            own_lanes = lanes(head * HALF_Q + t * HD, HD)
            bias = qb_ref[:, own_lanes]
            own_rows = pl.ds(t * pair_len + own_at, block_len)
            partner_rows = pl.ds(t * pair_len + partner_at, block_len)
            q_rows[h, own_rows, :] = (q_ref[h, :, own_lanes].astype(jnp.float32) + bias).astype(
                jnp.bfloat16
            )
            q_rows[h, partner_rows, :] = (
                other_ref[h * GROUP + t].astype(jnp.float32) + bias
            ).astype(jnp.bfloat16)
            d_rows[h, own_rows, :] = ct_ref[h, :, own_lanes]
            d_rows[h, partner_rows, :] = other_ref[(2 + h) * GROUP + t]
        d_cols[h] = jnp.transpose(d_rows[h].astype(jnp.float32)).astype(jnp.bfloat16)


def send_kernel(
    group_size, reach, me_ref, early_ref, late_ref, relay_ref, near_hbm, far_hbm, send_ref, all_ref, sem
):
    me = me_ref[0]
    all_ref[0] = early_ref[...]
    all_ref[1] = late_ref[...]
    all_ref[2] = relay_ref[...]
    copies = []
    for d in range(group_size):
        kind = route(me, jnp.int32(d), group_size, reach)
        copy = pltpu.make_async_copy(all_ref.at[kind, d % KVH], send_ref.at[d], sem.at[d])
        copy.start()
        copies.append(copy)
    for copy in copies:
        copy.wait()


def attention_kernel(
    group_size,
    reach,
    me_ref,
    len_ref,
    q_hbm,
    d_hbm,
    dt_hbm,
    other_hbm,
    kv_hbm,
    late_hbm,
    near_hbm,
    far_hbm,
    mine_hbm,
    back_hbm,
    parts_hbm,
    near_grad_hbm,
    far_grad_hbm,
    other_ref,
    mine_ref,
    back_ref,
    all_ref,
    stage_ref,
    win_ref,
    q_both,
    d_both,
    dt_both,
    p_ref,
    grad_ref,
    acc_ref,
    row_ref,
    sum_ref,
    in_sems,
    out_sems,
    tile_sems,
):
    block_len = mine_ref.shape[1]
    pair_len = 2 * block_len
    rows = GROUP * pair_len
    chunk = BLOCKS_PER_CHUNK * block_len
    scale = 1.0 / math.sqrt(HD)
    log2e = 1.0 / math.log(2.0)
    last_block = 2 * group_size - 1
    me = me_ref[0]
    head = me % 2
    pair = me - head
    n_docs = len_ref.shape[1]
    own_late, other_late, near, far = range(group_size, group_size + 4)

    loads = [
        pltpu.make_async_copy(source, into, in_sems.at[i])
        for i, (source, into) in enumerate(
            (
                (other_hbm.at[4 * GROUP :], other_ref),
                (kv_hbm, all_ref.at[:group_size]),
                (late_hbm.at[head], all_ref.at[own_late]),
                (near_hbm, all_ref.at[near]),
                (far_hbm, all_ref.at[far]),
                (q_hbm, q_both),
                (d_hbm, d_both),
                (dt_hbm, dt_both),
            )
        )
    ]
    for load in loads:
        load.start()

    def place(block):
        lowest_late = last_block - 1 - pair - reach
        doubled = jnp.where(
            group_size - 1 - block < pair - reach,
            group_size - 1 - block,
            jnp.where(block == lowest_late + head, near, far),
        )
        early = jnp.where(block <= pair + 1, block, doubled)
        c = last_block - block
        late = jnp.where(c == me, own_late, jnp.where(c == pair + 1 - head, other_late, c))
        return jnp.where(block < group_size, early, late)

    def tile_copies(first, count, sem):
        at = pl.ds(first, count)
        return [
            pltpu.make_async_copy(ref.at[at], hbm.at[at], tile_sems.at[i, sem])
            for i, (ref, hbm) in enumerate(((back_ref, back_hbm), (mine_ref, mine_hbm)))
        ]

    stage_ref[...] = jnp.zeros_like(stage_ref)
    sum_ref[...] = jnp.zeros_like(sum_ref)
    for load in loads[:6]:
        load.wait()
    all_ref[other_late, :, :HD] = other_ref[0]
    all_ref[other_late, :, HD:] = other_ref[1]

    def query_unit(h, carry):
        first_block = jnp.where(h == 0, pair, last_block - 1 - pair)
        first_pos = first_block * block_len
        own_at = pl.multiple_of(jnp.where(h == 0, head, 1 - head) * block_len, block_len)
        partner_at = pl.multiple_of(block_len - own_at, block_len)
        lane = lax.broadcasted_iota(jnp.int32, (1, rows), 1)
        query_pos = first_pos + lane % pair_len
        query_start = jnp.zeros_like(query_pos)
        end = jnp.int32(0)
        first_start = jnp.int32(0)
        for k in range(n_docs):
            end = end + len_ref[0, k]
            query_start = jnp.where(query_pos >= end, end, query_start)
            first_start = jnp.where(first_pos >= end, end, first_start)
        low = first_start // block_len
        n_blocks = first_block + 2 - low
        n_chunks = (n_blocks + BLOCKS_PER_CHUNK - 1) // BLOCKS_PER_CHUNK

        def load(i, carry):
            win_ref[pl.ds(pl.multiple_of(i * block_len, block_len), block_len), :] = all_ref[
                place(jnp.minimum(low + i, first_block + 1))
            ]
            return carry

        lax.fori_loop(0, n_chunks * BLOCKS_PER_CHUNK, load, 0)

        q_rows, d_rows = q_both.at[h], d_both.at[h]

        def window(i):
            return pl.ds(pl.multiple_of(i * chunk, chunk), chunk)

        def score_step(i, top):
            at = window(i)
            s = dot(win_ref[at, :HD], q_rows[...], NT) * (scale * log2e)
            key_pos = (low * block_len + i * chunk) + lax.broadcasted_iota(
                jnp.int32, (chunk, 1), 0
            )
            visible = (key_pos >= query_start) & (key_pos <= query_pos)
            s = jnp.where(visible, s, MASKED)
            p_ref[at, :] = s
            return jnp.maximum(top, jnp.max(s, axis=0, keepdims=True))

        top = lax.fori_loop(0, n_chunks, score_step, jnp.full((1, rows), MASKED, jnp.float32))

        acc_ref[...] = jnp.zeros_like(acc_ref)

        def out_step(i, total):
            at = window(i)
            e = jnp.exp2(p_ref[at, :] - top)
            p_ref[at, :] = e
            acc_ref[...] += dot(win_ref[at, HD:], e.astype(jnp.bfloat16), TN)
            return total + jnp.sum(e, axis=0, keepdims=True)

        total = lax.fori_loop(0, n_chunks, out_step, jnp.zeros((1, rows), jnp.float32))
        inverse = 1.0 / total

        @pl.when(h == 0)
        def _():
            for late_load in loads[6:]:
                late_load.wait()

        summed = acc_ref[...] * inverse
        delta = jnp.sum(summed * dt_both[h].astype(jnp.float32), axis=0, keepdims=True)
        row_ref[...] = jnp.transpose(summed)
        for t in range(GROUP):
            mine_ref[h * GROUP + t] = row_ref[
                pl.ds(t * pair_len + own_at, block_len), :
            ].astype(jnp.bfloat16)
            back_ref[h * GROUP + t] = row_ref[
                pl.ds(t * pair_len + partner_at, block_len), :
            ].astype(jnp.bfloat16)

        for copy in tile_copies(h * GROUP, GROUP, h):
            copy.start()
        acc_ref[...] = jnp.zeros_like(acc_ref)

        def grad_step(i, value_total):
            at = window(i)
            p = p_ref[at, :] * inverse
            dp = dot(win_ref[at, HD:], d_rows[...], NT)
            ds = (p * (dp - delta)).astype(jnp.bfloat16)
            value_part = dot(p.astype(jnp.bfloat16), d_rows[...], NN)
            grad_ref[at, HD:] = value_part
            grad_ref[at, :HD] = dot(ds, q_rows[...], NN) * scale
            acc_ref[...] += dot(win_ref[at, :HD], ds, TN)
            return value_total + jnp.sum(value_part, axis=0, keepdims=True)

        value_total = lax.fori_loop(0, n_chunks, grad_step, jnp.zeros((1, HD), jnp.float32))
        sum_ref[GROUP : GROUP + 1, :] += value_total
        row_ref[...] = jnp.transpose(acc_ref[...] * scale)
        for t in range(GROUP):
            mine_ref[(2 + h) * GROUP + t] = row_ref[
                pl.ds(t * pair_len + own_at, block_len), :
            ].astype(jnp.bfloat16)
            back_ref[(2 + h) * GROUP + t] = row_ref[
                pl.ds(t * pair_len + partner_at, block_len), :
            ].astype(jnp.bfloat16)
            sum_ref[t : t + 1, :] += jnp.sum(
                row_ref[t * pair_len : (t + 1) * pair_len, :], axis=0, keepdims=True
            )

        for copy in tile_copies((2 + h) * GROUP, GROUP, 2 + h):
            copy.start()

        def store(i, carry):
            slot = place(low + i)
            part = grad_ref[pl.ds(pl.multiple_of(i * block_len, block_len), block_len), :]
            stage_ref[slot, :block_len, :] = (
                stage_ref[slot, :block_len, :].astype(jnp.float32) + part
            ).astype(jnp.bfloat16)
            return carry

        lax.fori_loop(0, n_blocks, store, 0)
        return carry

    lax.fori_loop(0, 2, query_unit, 0)

    sums = sum_ref[...]
    high = sums.astype(jnp.bfloat16).astype(jnp.float32)
    middle = (sums - high).astype(jnp.bfloat16).astype(jnp.float32)
    lowest = sums - high - middle
    pieces = jnp.concatenate(
        [
            jnp.concatenate([high, middle], axis=1),
            jnp.concatenate([lowest, jnp.zeros_like(lowest)], axis=1),
        ],
        axis=0,
    ).astype(jnp.bfloat16)
    for d in range(group_size):
        stage_ref[d, block_len:, :] = pieces
    for ref, late in ((mine_ref, own_late), (back_ref, other_late)):
        ref[4 * GROUP] = stage_ref[late, :block_len, :HD]
        ref[4 * GROUP + 1] = stage_ref[late, :block_len, HD:]
    stores = [
        pltpu.make_async_copy(source, into, out_sems.at[i])
        for i, (source, into) in enumerate(
            (
                (stage_ref.at[near, :block_len], near_grad_hbm),
                (stage_ref.at[far, :block_len], far_grad_hbm),
                (stage_ref.at[:group_size], parts_hbm),
            )
        )
    ] + tile_copies(4 * GROUP, 2, 4)
    for store in stores:
        store.start()
    for i in range(4):
        stores += tile_copies(i * GROUP, GROUP, i)
    for store in stores:
        store.wait()


def join_kernel(
    me_ref, mine_ref, theirs_ref, near_hbm, far_hbm, att_ref, qg_ref, own_ref, theirs_late_ref
):
    head = me_ref[0] % 2
    for i, ref in enumerate((att_ref, qg_ref)):
        for h in range(2):
            for t in range(GROUP):
                tile = (2 * i + h) * GROUP + t
                ref[h, :, lanes(head * HALF_Q + t * HD, HD)] = mine_ref[tile]
                ref[h, :, lanes((1 - head) * HALF_Q + t * HD, HD)] = theirs_ref[tile]
    for ref, late_ref in ((mine_ref, own_ref), (theirs_ref, theirs_late_ref)):
        late_ref[:, :HD] = ref[4 * GROUP]
        late_ref[:, HD:] = ref[4 * GROUP + 1]


def total_kernel(
    group_size,
    reach,
    me_ref,
    got_ref,
    near_ref,
    far_ref,
    own_ref,
    theirs_ref,
    relay_ref,
    total_ref,
    sum_ref,
    acc_ref,
):
    block_len = total_ref.shape[2]
    me = me_ref[0]
    head = me % 2
    half = SUM_ROWS // 2
    acc_ref[2] = jnp.zeros_like(acc_ref[2])
    acc_ref[0, head] = near_ref[...].astype(jnp.float32)
    acc_ref[0, 1 - head] = far_ref[...].astype(jnp.float32)
    acc_ref[1, head] = own_ref[...].astype(jnp.float32)
    acc_ref[1, 1 - head] = theirs_ref[...].astype(jnp.float32)
    for d in range(group_size):
        kind = route(me, jnp.int32(d), group_size, reach)
        acc_ref[kind, d % KVH] += got_ref[d, :block_len, :].astype(jnp.float32)
    total_ref[...] = acc_ref[:2]
    relay_ref[...] = acc_ref[2].astype(jnp.bfloat16)
    for g in range(KVH):
        pieces = got_ref[g, block_len:, :].astype(jnp.float32)
        for d in range(g + KVH, group_size, KVH):
            pieces += got_ref[d, block_len:, :].astype(jnp.float32)
        sum_ref[g * half : (g + 1) * half, :] = (
            pieces[:half, :HD] + pieces[:half, HD:] + pieces[half:, :HD]
        )


def finish_kernel(total_ref, relay_ref, kg_ref, vg_ref):
    for g in range(KVH):
        cols = slice(g * HD, (g + 1) * HD)
        early = total_ref[0, g] + relay_ref[g].astype(jnp.float32)
        for h, total in enumerate((early, total_ref[1, g])):
            total = total.astype(jnp.bfloat16)
            kg_ref[h, :, cols] = total[:, :HD]
            vg_ref[h, :, cols] = total[:, HD:]


def bias_kernel(dp_ref, own_ref, *refs):
    *others, q_sum_ref, v_sum_ref, all_ref = refs
    me = dp_ref[0]
    for step, ref in enumerate((own_ref, *others)):
        all_ref[me ^ step] = ref[...]
    total = all_ref[0]
    for i in range(1, all_ref.shape[0]):
        total = total + all_ref[i]
    half = SUM_ROWS // 2
    for g in range(KVH):
        for t in range(GROUP):
            at = (g * GROUP + t) * HD
            q_sum_ref[:, at : at + HD] = total[g * half + t : g * half + t + 1]
        v_sum_ref[:, g * HD : (g + 1) * HD] = total[g * half + GROUP : (g + 1) * half]


def on_device(q_proj, k_proj, v_proj, q_bias, v_bias, cotangent, lengths):
    group_size = lax.axis_size("ctx")
    me = lax.axis_index("ctx").astype(jnp.int32)[None]
    q, ct, k, v = q_proj[0], cotangent[0], k_proj[0], v_proj[0]
    block_len = q.shape[1]
    reach = MOST // block_len
    rows = GROUP * 2 * block_len
    window = -(-(reach + 2) // BLOCKS_PER_CHUNK) * BLOCKS_PER_CHUNK * block_len
    bf16, f32 = jnp.bfloat16, jnp.float32
    more_tiles = jax.ShapeDtypeStruct((4 * GROUP + 2, block_len, HD), bf16)
    block = jax.ShapeDtypeStruct((block_len, SLOT_W), bf16)
    by_head = jax.ShapeDtypeStruct((KVH, block_len, SLOT_W), bf16)
    small = pltpu.CompilerParams(vmem_limit_bytes=SMALL_BYTES)
    large = pltpu.CompilerParams(vmem_limit_bytes=VMEM_BYTES)

    partners = [(i, i ^ 1) for i in range(group_size)]
    relays = [(i, group_size - 1 - i) for i in range(group_size - group_size // 4, group_size)]
    to_near, to_far = [], []
    for p in range(group_size // 2, group_size - group_size // 4, 2):
        lowest_late = 2 * group_size - 2 - p - reach
        for g in range(2):
            to_near.append((lowest_late + g, p + g))
            to_far.append((lowest_late + 1 - g, p + g))

    half_cols = (2, block_len, HALF_Q)
    row_pairs = jax.ShapeDtypeStruct((2, rows, HD), bf16)
    early, late, near, far = pl.pallas_call(
        blocks_kernel,
        out_shape=(by_head, by_head, block, block),
        in_specs=[SMEM] + [ANY] * 3,
        out_specs=(VMEM,) * 4,
        scratch_shapes=[
            pltpu.VMEM(k.shape, bf16),
            pltpu.VMEM(k.shape, bf16),
            pltpu.VMEM((1, KW), f32),
            pltpu.SemaphoreType.DMA((3,)),
        ],
        compiler_params=large,
        name="blocks",
    )(me, k, v, v_bias[None])
    relayed = lax.ppermute(early, "ctx", relays)
    near = lax.ppermute(near, "ctx", to_near)
    far = lax.ppermute(far, "ctx", to_far)
    swap = pl.pallas_call(
        swap_kernel,
        out_shape=more_tiles,
        in_specs=[SMEM, ANY, ANY, ANY],
        out_specs=VMEM,
        scratch_shapes=[
            pltpu.VMEM(half_cols, bf16),
            pltpu.VMEM(half_cols, bf16),
            pltpu.VMEM(block.shape, bf16),
            pltpu.SemaphoreType.DMA((3,)),
        ],
        compiler_params=large,
        cost_estimate=pl.CostEstimate(
            flops=SWAP_FLOPS, bytes_accessed=2_000_000, transcendentals=0
        ),
        name="swap",
    )(me, q, ct, late)
    other = lax.ppermute(swap, "ctx", partners)
    sent = pl.pallas_call(
        functools.partial(send_kernel, group_size, reach),
        out_shape=jax.ShapeDtypeStruct((group_size, block_len, SLOT_W), bf16),
        in_specs=[SMEM] + [VMEM] * 3 + [ANY] * 2,
        out_specs=ANY,
        scratch_shapes=[
            pltpu.VMEM((3, KVH, block_len, SLOT_W), bf16),
            pltpu.SemaphoreType.DMA((group_size,)),
        ],
        compiler_params=small,
        name="send",
    )(me, early, late, relayed, near, far)
    gathered = lax.all_to_all(sent, "ctx", 0, 0)
    q_rows, d_rows, d_cols = pl.pallas_call(
        prepare_kernel,
        out_shape=(row_pairs, row_pairs, jax.ShapeDtypeStruct((2, HD, rows), bf16)),
        in_specs=[SMEM] + [VMEM] * 4,
        out_specs=(VMEM,) * 3,
        cost_estimate=pl.CostEstimate(
            flops=PREP_FLOPS, bytes_accessed=4_000_000, transcendentals=0
        ),
        compiler_params=small,
        name="prepare",
    )(me, q, ct, other, q_bias[None])

    slot_len = block_len + SUM_ROWS
    mine, back, parts, near_grad, far_grad = pl.pallas_call(
        functools.partial(attention_kernel, group_size, reach),
        out_shape=(
            more_tiles,
            more_tiles,
            jax.ShapeDtypeStruct((group_size, slot_len, SLOT_W), bf16),
            block,
            block,
        ),
        in_specs=[SMEM, SMEM] + [ANY] * 8,
        out_specs=(ANY,) * 5,
        scratch_shapes=[
            pltpu.VMEM((2, block_len, HD), bf16),
            pltpu.VMEM(more_tiles.shape, bf16),
            pltpu.VMEM(more_tiles.shape, bf16),
            pltpu.VMEM((group_size + 4, block_len, SLOT_W), bf16),
            pltpu.VMEM((group_size + 4, slot_len, SLOT_W), bf16),
            pltpu.VMEM((window, SLOT_W), bf16),
            pltpu.VMEM(row_pairs.shape, bf16),
            pltpu.VMEM(row_pairs.shape, bf16),
            pltpu.VMEM((2, HD, rows), bf16),
            pltpu.VMEM((window, rows), f32),
            pltpu.VMEM((window, SLOT_W), f32),
            pltpu.VMEM((HD, rows), f32),
            pltpu.VMEM((rows, HD), f32),
            pltpu.VMEM((SUM_ROWS // 2, HD), f32),
            pltpu.SemaphoreType.DMA((8,)),
            pltpu.SemaphoreType.DMA((3,)),
            pltpu.SemaphoreType.DMA((2, 5)),
        ],
        compiler_params=large,
        cost_estimate=pl.CostEstimate(
            flops=3_000_000_000, bytes_accessed=10_000_000, transcendentals=2_000_000
        ),
        name="attention",
    )(me, lengths, q_rows, d_rows, d_cols, other, gathered, late, near, far)

    def back_along(pairs):
        return [(target, source) for source, target in pairs]

    theirs = lax.ppermute(back, "ctx", partners)
    near_grad = lax.ppermute(near_grad, "ctx", back_along(to_near))
    far_grad = lax.ppermute(far_grad, "ctx", back_along(to_far))
    got = lax.all_to_all(parts, "ctx", 0, 0)
    wide = jax.ShapeDtypeStruct(q.shape, bf16)
    narrow = jax.ShapeDtypeStruct(k.shape, bf16)
    attended, q_grad, own, theirs_late = pl.pallas_call(
        join_kernel,
        out_shape=(wide, wide, block, block),
        in_specs=[SMEM, VMEM, VMEM, ANY, ANY],
        out_specs=(VMEM,) * 4,
        cost_estimate=pl.CostEstimate(
            flops=JOIN_FLOPS, bytes_accessed=4_000_000, transcendentals=0
        ),
        compiler_params=small,
        name="join",
    )(me, mine, theirs, near_grad, far_grad)
    relay_total, total, sums = pl.pallas_call(
        functools.partial(total_kernel, group_size, reach),
        out_shape=(
            by_head,
            jax.ShapeDtypeStruct((2, KVH, block_len, SLOT_W), f32),
            jax.ShapeDtypeStruct((SUM_ROWS, HD), f32),
        ),
        in_specs=[SMEM] + [VMEM] * 5,
        out_specs=(VMEM, VMEM, VMEM),
        scratch_shapes=[pltpu.VMEM((3, KVH, block_len, SLOT_W), f32)],
        compiler_params=small,
        name="total",
    )(me, got, near_grad, far_grad, own, theirs_late)
    relay_grad = lax.ppermute(relay_total, "ctx", back_along(relays))
    dp_size = lax.axis_size("dp")
    dp_me = lax.axis_index("dp").astype(jnp.int32)[None]
    other_sums = [
        lax.ppermute(sums, "dp", [(i, i ^ step) for i in range(dp_size)])
        for step in range(1, dp_size)
    ]
    k_grad, v_grad = pl.pallas_call(
        finish_kernel,
        out_shape=(narrow, narrow),
        in_specs=[VMEM, VMEM],
        out_specs=(VMEM, VMEM),
        cost_estimate=pl.CostEstimate(
            flops=FINISH_FLOPS, bytes_accessed=1_000_000, transcendentals=0
        ),
        compiler_params=small,
        name="finish",
    )(total, relay_grad)
    q_sum, v_sum = pl.pallas_call(
        bias_kernel,
        out_shape=(jax.ShapeDtypeStruct((1, HQ), f32), jax.ShapeDtypeStruct((1, KW), f32)),
        in_specs=[SMEM] + [VMEM] * dp_size,
        out_specs=(VMEM, VMEM),
        scratch_shapes=[pltpu.VMEM((dp_size, SUM_ROWS, HD), f32)],
        cost_estimate=pl.CostEstimate(
            flops=BIAS_FLOPS, bytes_accessed=100_000, transcendentals=0
        ),
        compiler_params=small,
        name="bias",
    )(dp_me, sums, *other_sums)
    return (
        attended[None],
        q_grad[None],
        k_grad[None],
        v_grad[None],
        q_sum.reshape(HQ),
        v_sum.reshape(KW),
    )


def solution(mesh):
    placed = (
        P("dp", None, "ctx", None),
        P("dp", None, "ctx", None),
        P("dp", None, "ctx", None),
        P(),
        P(),
        P("dp", None, "ctx", None),
        P("dp", None),
    )
    return jax.shard_map(
        on_device,
        mesh=mesh,
        in_specs=placed,
        out_specs=(
            P("dp", None, "ctx", None),
            P("dp", None, "ctx", None),
            P("dp", None, "ctx", None),
            P("dp", None, "ctx", None),
            P(),
            P(),
        ),
        check_vma=False,
    )
```
